512 devices in a mesh: dp: 32 (over y_hi, z, core), tp: 16 (over y_lo, x).
Axes of the slice: x: 4, y: 8 (y_hi: 2, y_lo: 4; y = y_hi * 4 + y_lo), z: 8, core: 2. Of those that a mesh axis runs over, the one named last changes fastest.
Arguments:
- q_latent: bfloat16 [1024, 128, 576], P(('dp', 'tp')), may hold values from -160 to 160
- page_pool: bfloat16 [16384, 64, 576], P(('dp', 'tp')), may hold values from -6 to 6
- block_table: int32 [1024, 16], P(('dp', 'tp')), may hold values from 0 to 31, as said below
- cache_len: int32 [1024], P(('dp', 'tp')), may hold values from 1 to 1024
- prompt_of_row: int32 [1024], P(('dp', 'tp')), may hold values from 0 to 7
- prefix_cache: bfloat16 [32, 1024, 576], P('dp', 'tp'), may hold values from -6 to 6
- prefix_pages: int32 [8], replicated, may hold values from 1 to 16
- owners: int32 [8], replicated, may hold values from 0 to 31, as said below
Outputs:
- attended: bfloat16 [1024, 128, 512], P(('dp', 'tp'))
The draws below stay inside these ranges and needn't reach their ends.
Inputs may be any that keep to these rules, and one draw needn't show every extreme that they name: `block_table`: each device's rows name its own pages: the entries of its 2 rows together are every number below 32 once. `owners`: distinct ranks.
All inputs are finite; a program needn't handle non-finite values.
Results may differ from the reference program's by a relative error of at most 0.009.
Values may be sent and summed in bfloat16 or wider, within the bound.
A program may use at most 64 MiB of HBM per device.

```python
import jax
import jax.numpy as jnp
from jax import lax

HEADS = 128
LAT = 512
ROPE = 64
R_DEV = 2
PAGE = 64
MAXP = 16
PROMPTS = 8
PFX_PAGES = 16
ROWS = 1024
POOL = 16384
OWNER_SLOTS = 32


def cache_values(key, count, tokens):
    width = LAT + ROPE
    values = jax.random.normal(key, (count, tokens, width), jnp.float32)
    return jnp.clip(values, -6.0, 6.0)


def draw_page_pool(key, part):
    key = jax.random.fold_in(key, 11)
    values = cache_values(key, POOL, PAGE)
    return values.astype(jnp.bfloat16)


def draw_prefix_cache(key, part):
    key = jax.random.fold_in(key, 12)
    values = cache_values(key, OWNER_SLOTS, PFX_PAGES * PAGE)
    return values.astype(jnp.bfloat16)


def draw_q_latent(key, part):
    key = jax.random.fold_in(key, 13)
    width = LAT + ROPE
    values = jnp.clip(jax.random.normal(key, (ROWS, HEADS, width), jnp.float32), -6.0, 6.0)
    return values.astype(jnp.bfloat16)


def draw_block_table(key, part):
    key = jax.random.fold_in(key, 21)
    devices = ROWS // R_DEV
    keys = jax.random.split(key, devices)
    orders = jax.vmap(lambda single: jax.random.permutation(single, R_DEV * MAXP))(keys)
    return orders.reshape(ROWS, MAXP).astype(jnp.int32)


def draw_cache_len(key, part):
    key = jax.random.fold_in(key, 22)
    lengths = jax.random.randint(key, (ROWS,), 1, MAXP * PAGE + 1)
    longest = jax.random.randint(jax.random.fold_in(key, 1), (), 0, ROWS)
    return lengths.at[longest].set(MAXP * PAGE).astype(jnp.int32)


def draw_prefix_pages(key, part):
    key = jax.random.fold_in(key, 23)
    counts = jax.random.randint(key, (PROMPTS,), 1, PFX_PAGES + 1)
    longest = jax.random.randint(jax.random.fold_in(key, 1), (), 0, PROMPTS)
    return counts.at[longest].set(PFX_PAGES).astype(jnp.int32)


def draw_owners(key, part):
    key = jax.random.fold_in(key, 24)
    return jax.random.permutation(key, OWNER_SLOTS)[:PROMPTS].astype(jnp.int32)


def with_ends(entries, own_key, least, top_value):
    place = [jax.random.randint(jax.random.fold_in(own_key, axis), (), 0, length) for axis, length in enumerate(entries.shape)]
    widest = entries.shape.index(max(entries.shape))
    beside = place[:widest] + [(place[widest] + 1) % entries.shape[widest]] + place[widest + 1:]
    return entries.at[tuple(place)].set(least).at[tuple(beside)].set(top_value)


def setup_inputs(seed: int = 0) -> dict:
    arg_keys = jax.random.split(jax.random.key(seed), 9)
    q_latent = draw_q_latent(jax.random.fold_in(arg_keys[8], 71), 0)
    page_pool = draw_page_pool(jax.random.fold_in(arg_keys[8], 71), 0)
    block_table = draw_block_table(jax.random.fold_in(arg_keys[8], 71), 0)
    cache_len = draw_cache_len(jax.random.fold_in(arg_keys[8], 71), 0)
    prompt_of_row = with_ends(jax.random.randint(arg_keys[4], (ROWS,), 0, PROMPTS), jax.random.fold_in(arg_keys[4], 1), 0, PROMPTS - 1).astype(jnp.int32)
    prefix_cache = draw_prefix_cache(jax.random.fold_in(arg_keys[8], 71), 0)
    prefix_pages = draw_prefix_pages(jax.random.fold_in(arg_keys[8], 71), 0)
    owners = draw_owners(jax.random.fold_in(arg_keys[8], 71), 0)
    return {"q_latent": q_latent, "page_pool": page_pool, "block_table": block_table, "cache_len": cache_len, "prompt_of_row": prompt_of_row, "prefix_cache": prefix_cache, "prefix_pages": prefix_pages, "owners": owners}


softmax_scale = 192.0 ** -0.5


def reference(q_latent, page_pool, block_table, cache_len, prompt_of_row, prefix_cache, prefix_pages, owners):
    rows = q_latent.shape[0]
    device_of = jnp.arange(rows, dtype=jnp.int32) // R_DEV
    global_pages = (block_table + (device_of * (R_DEV * MAXP))[:, None]).astype(jnp.int32)
    prefix_keys = prefix_cache[owners]
    prefix_tokens = prefix_cache.shape[1]
    prefix_valid = jnp.arange(prefix_tokens, dtype=jnp.int32)[None, :] < (prefix_pages * PAGE)[:, None]
    width = LAT + ROPE

    def one_row(items):
        query, pages, length, prompt = items
        private = page_pool[pages].reshape(MAXP * PAGE, width)
        private_ok = jnp.arange(MAXP * PAGE, dtype=jnp.int32) < length
        keys = jnp.concatenate([private, prefix_keys[prompt]], 0)
        valid = jnp.concatenate([private_ok, prefix_valid[prompt]], 0)
        score = jnp.einsum("hk,tk->ht", query.astype(jnp.float32), keys.astype(jnp.float32)) * softmax_scale
        score = jnp.where(valid[None, :], score, -1e30)
        peak = jnp.max(score, axis=-1, keepdims=True)
        weight = jnp.where(valid[None, :], jnp.exp(score - peak), 0.0)
        total = jnp.sum(weight, axis=-1)
        rounded = lax.optimization_barrier(weight.astype(jnp.bfloat16))
        numerator = jnp.einsum("ht,tv->hv", rounded.astype(jnp.float32), keys[:, :LAT].astype(jnp.float32))
        return (numerator / total[:, None]).astype(jnp.bfloat16)

    return lax.map(one_row, (q_latent, global_pages, cache_len, prompt_of_row))
```

```python
import jax
import jax.numpy as jnp
from jax import lax
from jax.experimental import pallas as pl
from jax.experimental.pallas import tpu as pltpu
from jax.sharding import PartitionSpec as P

LAT = 512
ROPE = 64
WIDTH = LAT + ROPE
HEADS = 128
PAGE = 64
MAXP = 16
PROMPTS = 8
ROWS_DEV = 2
X, Y, Z, DP, TP = 4, 4, 8, 32, 16
NEAR = 2 * Z
POS = PROMPTS + 1
SCALE = 192.0 ** (-0.5)
BIG_NEGATIVE = -1e30
MESH = pl.DeviceIdType.MESH
TN = (((0,), (0,)), ((), ()))
NN = (((1,), (0,)), ((), ()))


def kernel(
    table_hbm, length_hbm, prompt_hbm, pages_hbm, owners_hbm, queries_hbm, slot_hbm, pool_hbm, out,
    table, length, prompt, pages, owners, queries, slot, gathered, received, picked, traded, staged, pool, others, other_block,
    other_prompt, partial, arrived, numer, stats,
    local_sem, prompt_sem, p1_send, p1_recv, z_send, z_recv, t_send, t_recv, r_send, r_recv, c_send, c_recv,
):
    dp = lax.axis_index("dp")
    tp = lax.axis_index("tp")
    core = dp % 2
    z = (dp // 2) % Z
    y_hi = dp // (2 * Z)
    y_lo = tp // X
    x = tp % X
    twin = (dp + 1 - 2 * core, tp)

    def at_y(step):
        y = (y_hi * Y + y_lo + step + 2 * Y) % (2 * Y)
        return (((y // Y) * Z + z) * 2 + core, (y % Y) * X + x)

    def at_x(step):
        return (dp, y_lo * X + (x + step + X) % X)

    def at_z(step):
        return ((y_hi * Z + (z + step + Z) % Z) * 2 + core, tp)

    slot_copy, query_in, pool_copy, *small_copies = [
        pltpu.make_async_copy(source, target, local_sem.at[i])
        for i, (source, target) in enumerate((
            (slot_hbm, slot), (queries_hbm, queries), (pool_hbm, pool), (owners_hbm, owners),
            (prompt_hbm, prompt), (pages_hbm, pages), (table_hbm, table), (length_hbm, length),
        ))
    ]
    for copy in [slot_copy, query_in, pool_copy] + small_copies:
        copy.start()

    barrier = pltpu.get_barrier_semaphore()

    def near(i):
        return y_hi * NEAR + (dp + i) % NEAR

    partner = ((1 - y_hi) * NEAR + dp % NEAR, tp)

    @pl.loop(1, NEAR)
    def _(i):
        pl.semaphore_signal(barrier, inc=1, device_id=(near(i), tp), device_id_type=MESH)

    pl.semaphore_signal(barrier, inc=1, device_id=partner, device_id_type=MESH)

    @pl.loop(1, TP)
    def _(i):
        pl.semaphore_signal(barrier, inc=1, device_id=(dp, (tp + i) % TP), device_id_type=MESH)

    for step in (1, -1):
        pl.semaphore_signal(barrier, inc=1, device_id=at_y(step), device_id_type=MESH)

    slot_copy.wait()

    for half in range(2):
        low = slot[0, 32 * half : 32 * half + 16, LAT:WIDTH]
        high = slot[0, 32 * half + 16 : 32 * half + 32, LAT:WIDTH]
        rotary = jnp.concatenate([low, high], axis=1)
        for tile in range(Z):
            lanes, tokens = tile // 2, tile % 2
            first = 32 * half + 16 * tokens
            staged[half, tile, 0] = slot[0, first : first + 16, 128 * lanes : 128 * lanes + 128]
            staged[half, tile, 1] = rotary

    pl.semaphore_wait(barrier, NEAR - 1 + 1 + TP - 1 + 2)

    def remote(src, dst, send, recv, device):
        return pltpu.make_async_remote_copy(
            src_ref=src, dst_ref=dst, send_sem=send, recv_sem=recv, device_id=device, device_id_type=MESH
        )

    def spread(i):
        to = near(i)
        return remote(
            staged.at[to % 2, (to // 2) % Z], received.at[dp % NEAR], p1_send.at[i], p1_recv.at[i], (to, tp)
        )

    def spread_in(i):
        source = (dp - i + DP) % NEAR
        return remote(
            staged.at[0, 0], received.at[source], p1_send.at[i], p1_recv.at[i], (near(i), tp)
        )

    @pl.loop(1, NEAR)
    def _(i):
        spread(i).start()

    received[dp % NEAR] = staged[core, z]
    prompt_copy = remote(prompt_hbm, other_block, c_send.at[0], c_recv.at[0], twin)
    prompt_copy.start()
    query_copy = remote(queries_hbm, others, c_send.at[1], c_recv.at[1], twin)
    query_copy.start()
    for copy in [query_in] + small_copies:
        copy.wait()

    token = lax.broadcasted_iota(jnp.int32, (4 * PAGE, HEADS), 0)

    def turned_wide(line):
        return jnp.transpose(jnp.broadcast_to(line, (HEADS, HEADS)))

    def attend(scores, values):
        peak = jnp.max(scores[0], axis=0, keepdims=True)
        for score in scores[1:]:
            peak = jnp.maximum(peak, jnp.max(score, axis=0, keepdims=True))
        total = jnp.zeros((1, HEADS), jnp.float32)
        numerator = jnp.zeros((HEADS, LAT), jnp.float32)
        for score, value in zip(scores, values):
            weight = jnp.exp(score - peak)
            total = total + jnp.sum(weight, axis=0, keepdims=True)
            numerator = numerator + lax.dot_general(
                weight.astype(jnp.bfloat16), value(), TN, preferred_element_type=jnp.float32
            )
        return turned_wide(peak), turned_wide(total), numerator

    def private(row):
        limit = length[row]

        def block(number):
            return jnp.concatenate([pool[table[row, 4 * number + i]] for i in range(4)], axis=0)

        scores = []
        for number in range(4):
            score = lax.dot_general(block(number), queries[row], NN, preferred_element_type=jnp.float32)
            scores.append(jnp.where(token + 256 * number < limit, score * SCALE, BIG_NEGATIVE))
        peak, total, numerator = attend(
            scores, [lambda number=number: block(number)[:, :LAT] for number in range(4)]
        )
        numer[row] = numerator
        stats[row, 0] = peak
        stats[row, 1] = total

    pool_copy.wait()
    for row in range(ROWS_DEV):
        private(row)

    @pl.loop(1, NEAR)
    def _(i):
        spread_in(i).wait_recv()

    for p in range(PROMPTS):
        picked[p] = received[owners[p] % NEAR, 0]
    picked[PROMPTS] = received[owners[z] % NEAR, 1]
    trade = remote(picked, traded, c_send.at[4], c_recv.at[4], partner)
    trade.start()
    trade.wait_recv()
    for p in range(POS):
        owner = owners[p] if p < PROMPTS else owners[z]
        gathered[y_lo, x, z, p] = jnp.where(owner // NEAR == y_hi, picked[p], traded[p])

    def z_out(i):
        mine = gathered.at[y_lo, x, z, 0:6]
        return remote(mine, mine, z_send.at[i], z_recv.at[i], at_z(i))

    def z_in(i):
        theirs = gathered.at[y_lo, x, (z - i + Z) % Z, 0:6]
        return remote(theirs, theirs, z_send.at[i], z_recv.at[i], at_z(i))

    def t_out(i):
        mine = gathered.at[y_lo, x, z, 6:9]
        return remote(mine, mine, t_send.at[i], t_recv.at[i], (dp, (tp + i) % TP))

    def t_in(i):
        source = (tp - i + TP) % TP
        theirs = gathered.at[source // X, source % X, z, 6:9]
        return remote(theirs, theirs, t_send.at[i], t_recv.at[i], (dp, (tp + i) % TP))

    @pl.loop(1, Z)
    def _(i):
        z_out(i).start()

    @pl.loop(1, TP)
    def _(i):
        t_out(i).start()

    prompt_copy.wait_recv()
    to_scalar = pltpu.make_async_copy(other_block, other_prompt, prompt_sem)
    to_scalar.start()
    to_scalar.wait()

    started = []

    class Ring:
        def __init__(self, half, place, device, first, size, steps):
            self.half, self.place, self.device = half, place, device
            self.first, self.size, self.steps = first, size, steps

        def copy(self, step, number, way, behind):
            sign = 1 - 2 * way
            origin = (self.place - sign * behind + 2 * self.size) % self.size
            ref = self.half(origin, number if way == 0 else 1 - number)
            index = self.first + 2 * (2 * (step - 1) + number) + way
            return remote(ref, ref, r_send.at[index], r_recv.at[index], self.device(sign))

        def send(self, step, number):
            for way in range(2):
                copy = self.copy(step, number, way, step - 1)
                copy.start()
                started.append(copy)

        def begin(self):
            self.send(1, 0)
            self.send(1, 1)

        def land(self, step, number):
            forward = step + 1 < self.steps or (step + 1 == self.steps and number == 0)
            for way in range(2):
                self.copy(step, number, way, step).wait_recv()
                if forward:
                    copy = self.copy(step + 1, number, way, step)
                    copy.start()
                    started.append(copy)

    ay = Ring(lambda y, h: gathered.at[y, x, 4 * h : 4 * h + 4, 0:3], y_lo, at_y, 0, Y, 2)
    bx = Ring(lambda at, h: gathered.at[y_lo, at, 4 * h : 4 * h + 4, 3:6], x, at_x, 6, X, 2)
    ax = Ring(lambda at, h: gathered.at[2 * h : 2 * h + 2, at, :, 0:3], x, at_x, 12, X, 2)
    by = Ring(lambda y, h: gathered.at[y, 2 * h : 2 * h + 2, :, 3:6], y_lo, at_y, 18, Y, 2)
    cz = Ring(lambda at, h: gathered.at[2 * h : 2 * h + 2, :, at, 6:9], z, at_z, 24, Z, 4)

    @pl.loop(1, Z)
    def _(i):
        z_in(i).wait_recv()

    ay.begin()
    bx.begin()

    @pl.loop(1, TP)
    def _(i):
        t_in(i).wait_recv()

    cz.begin()
    ay.land(1, 0)
    bx.land(1, 0)
    ay.land(1, 1)
    bx.land(1, 1)
    cz.land(1, 0)
    ay.land(2, 0)
    ax.begin()
    bx.land(2, 0)
    by.begin()
    cz.land(1, 1)
    cz.land(2, 0)
    ax.land(1, 0)
    by.land(1, 0)
    cz.land(2, 1)
    cz.land(3, 0)
    ax.land(1, 1)
    by.land(1, 1)
    query_copy.wait_recv()
    cz.land(3, 1)
    cz.land(4, 0)
    ax.land(2, 0)
    by.land(2, 0)

    page_of = lax.broadcasted_iota(jnp.int32, (256, HEADS), 0) // 16
    blank = jnp.zeros((ROPE, HEADS), jnp.bfloat16)

    def prefix(query, p):
        limit = pages[p]
        latent, rotary = query[:LAT], query[LAT:]
        keys = [
            jnp.concatenate(
                [gathered[:, :, 2 * lanes + tokens, p].reshape(256, 128) for lanes in range(4)], axis=1
            )
            for tokens in range(2)
        ]
        packed = gathered[:, :, p, PROMPTS].reshape(256, 128)
        scores = []
        for tokens in range(2):
            parts = [rotary, blank] if tokens == 0 else [blank, rotary]
            score = lax.dot_general(keys[tokens], latent, NN, preferred_element_type=jnp.float32)
            score = score + lax.dot_general(
                packed, jnp.concatenate(parts, axis=0), NN, preferred_element_type=jnp.float32
            )
            scores.append(jnp.where(page_of < limit, score * SCALE, BIG_NEGATIVE))
        return attend(scores, [lambda key=key: key for key in keys])

    returns = []
    for row in range(ROWS_DEV):
        peak, total, numerator = prefix(others[row], other_prompt[row])
        partial[row, :, :LAT] = numerator
        partial[row, :, LAT : LAT + 128] = peak
        partial[row, :, LAT + 128 :] = total
        back = remote(partial.at[row], arrived.at[row], c_send.at[2 + row], c_recv.at[2 + row], twin)
        back.start()
        returns.append(back)

    for row in range(ROWS_DEV):
        peak, total, numerator = prefix(queries[row], prompt[row])
        returns[row].wait_recv()
        m0, t0 = stats[row, 0], stats[row, 1]
        m1, t1 = arrived[row, :, LAT : LAT + 128], arrived[row, :, LAT + 128 :]
        top = jnp.maximum(jnp.maximum(peak, m0), m1)
        f, f0, f1 = jnp.exp(peak - top), jnp.exp(m0 - top), jnp.exp(m1 - top)
        whole = total * f + t0 * f0 + t1 * f1
        f, f0, f1 = f / whole, f0 / whole, f1 / whole
        for lanes in range(0, LAT, 128):
            part = slice(lanes, lanes + 128)
            summed = numerator[:, part] * f + numer[row, :, part] * f0 + arrived[row, :, part] * f1
            out[row, :, part] = summed.astype(out.dtype)

    @pl.loop(1, NEAR)
    def _(i):
        spread(i).wait_send()

    @pl.loop(1, Z)
    def _(i):
        z_out(i).wait_send()

    @pl.loop(1, TP)
    def _(i):
        t_out(i).wait_send()

    for copy in started + [trade, prompt_copy, query_copy] + returns:
        copy.wait_send()


def on_device(
    q_latent, page_pool, block_table, cache_len, prompt_of_row, prefix_cache, prefix_pages, owners
):
    anywhere = pl.BlockSpec(memory_space=pl.ANY)
    i32 = jnp.int32
    bf16, f32 = jnp.bfloat16, jnp.float32
    dma = pltpu.SemaphoreType.DMA
    return pl.pallas_call(
        kernel,
        out_shape=jax.ShapeDtypeStruct((ROWS_DEV, HEADS, LAT), bf16),
        in_specs=[anywhere] * 8,
        out_specs=pl.BlockSpec(memory_space=pltpu.VMEM),
        scratch_shapes=[
            pltpu.SMEM((ROWS_DEV, MAXP), i32),
            pltpu.SMEM((ROWS_DEV,), i32),
            pltpu.SMEM((ROWS_DEV,), i32),
            pltpu.SMEM((PROMPTS,), i32),
            pltpu.SMEM((PROMPTS,), i32),
            pltpu.VMEM((ROWS_DEV, WIDTH, HEADS), bf16),
            pltpu.VMEM((1, PAGE, WIDTH), bf16),
            pltpu.VMEM((Y, X, Z, POS, 16, 128), bf16),
            pltpu.VMEM((NEAR, 2, 16, 128), bf16),
            pltpu.VMEM((POS, 16, 128), bf16),
            pltpu.VMEM((POS, 16, 128), bf16),
            pltpu.VMEM((2, Z, 2, 16, 128), bf16),
            pltpu.VMEM((ROWS_DEV * MAXP, PAGE, WIDTH), bf16),
            pltpu.VMEM((ROWS_DEV, WIDTH, HEADS), bf16),
            pltpu.VMEM((ROWS_DEV,), i32),
            pltpu.SMEM((ROWS_DEV,), i32),
            pltpu.VMEM((ROWS_DEV, HEADS, LAT + 256), f32),
            pltpu.VMEM((ROWS_DEV, HEADS, LAT + 256), f32),
            pltpu.VMEM((ROWS_DEV, HEADS, LAT), f32),
            pltpu.VMEM((ROWS_DEV, 2, HEADS, 128), f32),
            dma((8,)), dma,
            dma((NEAR,)), dma((NEAR,)),
            dma((Z,)), dma((Z,)),
            dma((TP,)), dma((TP,)),
            dma((38,)), dma((38,)),
            dma((5,)), dma((5,)),
        ],
        compiler_params=pltpu.CompilerParams(
            collective_id=0, has_side_effects=True, vmem_limit_bytes=60 * 1024 * 1024
        ),
        cost_estimate=pl.CostEstimate(flops=1200000000, bytes_accessed=3000000, transcendentals=600000),
    )(
        block_table, cache_len, prompt_of_row, prefix_pages, owners,
        jnp.swapaxes(q_latent, 1, 2), prefix_cache, page_pool,
    )


def solution(mesh):
    placed = (
        P(("dp", "tp"), None, None),
        P(("dp", "tp"), None, None),
        P(("dp", "tp"), None),
        P(("dp", "tp")),
        P(("dp", "tp")),
        P("dp", "tp", None),
        P(),
        P(),
    )
    return jax.shard_map(
        on_device,
        mesh=mesh,
        in_specs=placed,
        out_specs=P(("dp", "tp"), None, None),
        check_vma=False,
    )
```

```python
import jax
import jax.numpy as jnp
from jax import lax
from jax.experimental import pallas as pl
from jax.experimental.pallas import tpu as pltpu
from jax.sharding import PartitionSpec as P

LAT = 512
ROPE = 64
WIDTH = LAT + ROPE
HEADS = 128
PAGE = 64
MAXP = 16
PROMPTS = 8
ROWS_DEV = 2
X, Y, Z, DP, TP = 4, 4, 8, 32, 16
NEAR = 2 * Z
POS = PROMPTS + 1
SCALE = 192.0 ** (-0.5)
BIG_NEGATIVE = -1e30
MESH = pl.DeviceIdType.MESH
TN = (((0,), (0,)), ((), ()))
NN = (((1,), (0,)), ((), ()))


def kernel(
    table_hbm, length_hbm, prompt_hbm, pages_hbm, owners_hbm, queries_hbm, slot_hbm, pool_hbm, out,
    table, length, prompt, pages, owners, queries, slot, gathered, received, picked, traded, staged, pool, others, other_block,
    other_prompt, partial, arrived, numer, stats,
    local_sem, prompt_sem, p1_send, p1_recv, z_send, z_recv, t_send, t_recv, r_send, r_recv, c_send, c_recv,
):
    dp = lax.axis_index("dp")
    tp = lax.axis_index("tp")
    core = dp % 2
    z = (dp // 2) % Z
    y_hi = dp // (2 * Z)
    y_lo = tp // X
    x = tp % X
    twin = (dp + 1 - 2 * core, tp)

    def at_y(step):
        y = (y_hi * Y + y_lo + step + 2 * Y) % (2 * Y)
        return (((y // Y) * Z + z) * 2 + core, (y % Y) * X + x)

    def at_x(step):
        return (dp, y_lo * X + (x + step + X) % X)

    def at_z(step):
        return ((y_hi * Z + (z + step + Z) % Z) * 2 + core, tp)

    slot_copy, query_in, pool_copy, *small_copies = [
        pltpu.make_async_copy(source, target, local_sem.at[i])
        for i, (source, target) in enumerate((
            (slot_hbm, slot), (queries_hbm, queries), (pool_hbm, pool), (owners_hbm, owners),
            (prompt_hbm, prompt), (pages_hbm, pages), (table_hbm, table), (length_hbm, length),
        ))
    ]
    for copy in [slot_copy, query_in, pool_copy] + small_copies:
        copy.start()

    barrier = pltpu.get_barrier_semaphore()

    def near(i):
        return y_hi * NEAR + (dp + i) % NEAR

    partner = ((1 - y_hi) * NEAR + dp % NEAR, tp)

    @pl.loop(1, NEAR)
    def _(i):
        pl.semaphore_signal(barrier, inc=1, device_id=(near(i), tp), device_id_type=MESH)

    pl.semaphore_signal(barrier, inc=1, device_id=partner, device_id_type=MESH)

    @pl.loop(1, TP)
    def _(i):
        pl.semaphore_signal(barrier, inc=1, device_id=(dp, (tp + i) % TP), device_id_type=MESH)

    for step in (1, -1):
        pl.semaphore_signal(barrier, inc=1, device_id=at_y(step), device_id_type=MESH)

    slot_copy.wait()

    for half in range(2):
        low = slot[0, 32 * half : 32 * half + 16, LAT:WIDTH]
        high = slot[0, 32 * half + 16 : 32 * half + 32, LAT:WIDTH]
        rotary = jnp.concatenate([low, high], axis=1)
        for tile in range(Z):
            lanes, tokens = tile // 2, tile % 2
            first = 32 * half + 16 * tokens
            staged[half, tile, 0] = slot[0, first : first + 16, 128 * lanes : 128 * lanes + 128]
            staged[half, tile, 1] = rotary

    pl.semaphore_wait(barrier, NEAR - 1 + 1 + TP - 1 + 2)

    def remote(src, dst, send, recv, device):
        return pltpu.make_async_remote_copy(
            src_ref=src, dst_ref=dst, send_sem=send, recv_sem=recv, device_id=device, device_id_type=MESH
        )

    def spread(i):
        to = near(i)
        return remote(
            staged.at[to % 2, (to // 2) % Z], received.at[dp % NEAR], p1_send.at[i], p1_recv.at[i], (to, tp)
        )

    def spread_in(i):
        source = (dp - i + DP) % NEAR
        return remote(
            staged.at[0, 0], received.at[source], p1_send.at[i], p1_recv.at[i], (near(i), tp)
        )

    @pl.loop(1, NEAR)
    def _(i):
        spread(i).start()

    received[dp % NEAR] = staged[core, z]
    prompt_copy = remote(prompt_hbm, other_block, c_send.at[0], c_recv.at[0], twin)
    prompt_copy.start()
    query_copy = remote(queries_hbm, others, c_send.at[1], c_recv.at[1], twin)
    query_copy.start()
    for copy in [query_in] + small_copies:
        copy.wait()

    token = lax.broadcasted_iota(jnp.int32, (4 * PAGE, HEADS), 0)

    def turned_wide(line):
        return jnp.transpose(jnp.broadcast_to(line, (HEADS, HEADS)))

    def attend(scores, values):
        peak = jnp.max(scores[0], axis=0, keepdims=True)
        for score in scores[1:]:
            peak = jnp.maximum(peak, jnp.max(score, axis=0, keepdims=True))
        total = jnp.zeros((1, HEADS), jnp.float32)
        numerator = jnp.zeros((HEADS, LAT), jnp.float32)
        for score, value in zip(scores, values):
            weight = jnp.exp(score - peak)
            total = total + jnp.sum(weight, axis=0, keepdims=True)
            numerator = numerator + lax.dot_general(
                weight.astype(jnp.bfloat16), value(), TN, preferred_element_type=jnp.float32
            )
        return turned_wide(peak), turned_wide(total), numerator

    def private(row):
        limit = length[row]

        def block(number):
            return jnp.concatenate([pool[table[row, 4 * number + i]] for i in range(4)], axis=0)

        scores = []
        for number in range(4):
            score = lax.dot_general(block(number), queries[row], NN, preferred_element_type=jnp.float32)
            scores.append(jnp.where(token + 256 * number < limit, score * SCALE, BIG_NEGATIVE))
        peak, total, numerator = attend(
            scores, [lambda number=number: block(number)[:, :LAT] for number in range(4)]
        )
        numer[row] = numerator
        stats[row, 0] = peak
        stats[row, 1] = total

    pool_copy.wait()
    for row in range(ROWS_DEV):
        private(row)

    @pl.loop(1, NEAR)
    def _(i):
        spread_in(i).wait_recv()

    for p in range(PROMPTS):
        picked[p] = received[owners[p] % NEAR, 0]
    picked[PROMPTS] = received[owners[z] % NEAR, 1]
    trade = remote(picked, traded, c_send.at[4], c_recv.at[4], partner)
    trade.start()
    trade.wait_recv()
    for p in range(POS):
        owner = owners[p] if p < PROMPTS else owners[z]
        gathered[y_lo, x, z, p] = jnp.where(owner // NEAR == y_hi, picked[p], traded[p])

    def z_out(i):
        mine = gathered.at[y_lo, x, z, 0:6]
        return remote(mine, mine, z_send.at[i], z_recv.at[i], at_z(i))

    def z_in(i):
        theirs = gathered.at[y_lo, x, (z - i + Z) % Z, 0:6]
        return remote(theirs, theirs, z_send.at[i], z_recv.at[i], at_z(i))

    def t_out(i):
        mine = gathered.at[y_lo, x, z, 6:9]
        return remote(mine, mine, t_send.at[i], t_recv.at[i], (dp, (tp + i) % TP))

    def t_in(i):
        source = (tp - i + TP) % TP
        theirs = gathered.at[source // X, source % X, z, 6:9]
        return remote(theirs, theirs, t_send.at[i], t_recv.at[i], (dp, (tp + i) % TP))

    @pl.loop(1, Z)
    def _(i):
        z_out(i).start()

    @pl.loop(1, TP)
    def _(i):
        t_out(i).start()

    prompt_copy.wait_recv()
    to_scalar = pltpu.make_async_copy(other_block, other_prompt, prompt_sem)
    to_scalar.start()
    to_scalar.wait()

    started = []

    class Ring:
        def __init__(self, half, place, device, first, size, steps):
            self.half, self.place, self.device = half, place, device
            self.first, self.size, self.steps = first, size, steps

        def copy(self, step, number, way, behind):
            sign = 1 - 2 * way
            origin = (self.place - sign * behind + 2 * self.size) % self.size
            ref = self.half(origin, number if way == 0 else 1 - number)
            index = self.first + 2 * (2 * (step - 1) + number) + way
            return remote(ref, ref, r_send.at[index], r_recv.at[index], self.device(sign))

        def send(self, step, number):
            for way in range(2):
                copy = self.copy(step, number, way, step - 1)
                copy.start()
                started.append(copy)

        def begin(self):
            self.send(1, 0)
            self.send(1, 1)

        def land(self, step, number):
            forward = step + 1 < self.steps or (step + 1 == self.steps and number == 0)
            for way in range(2):
                self.copy(step, number, way, step).wait_recv()
                if forward:
                    copy = self.copy(step + 1, number, way, step)
                    copy.start()
                    started.append(copy)

    ay = Ring(lambda y, h: gathered.at[y, x, 4 * h : 4 * h + 4, 0:3], y_lo, at_y, 0, Y, 2)
    bx = Ring(lambda at, h: gathered.at[y_lo, at, 4 * h : 4 * h + 4, 3:6], x, at_x, 6, X, 2)
    class Slab:
        def __init__(self, piece, place, device, first):
            self.piece, self.place, self.device, self.first = piece, place, device, first

        def copy(self, step, way, behind):
            sign = 1 - 2 * way
            origin = (self.place - sign * behind + 8) % 4
            ref = self.piece(origin, pl.ds(0, Z) if step == 1 else pl.ds(4 * way, 4))
            index = self.first + 2 * (step - 1) + way
            return remote(ref, ref, r_send.at[index], r_recv.at[index], self.device(sign))

        def begin(self):
            for way in range(2):
                copy = self.copy(1, way, 0)
                copy.start()
                started.append(copy)

        def land(self):
            for way in range(2):
                self.copy(1, way, 1).wait_recv()
                copy = self.copy(2, way, 1)
                copy.start()
                started.append(copy)

        def finish(self):
            for way in range(2):
                self.copy(2, way, 2).wait_recv()

    def slab_x(offset):
        row = (y_lo + offset) % Y
        return Slab(lambda at, zs: gathered.at[row, at, zs, 0:3], x, at_x, 26 + 4 * offset)

    def slab_y(offset):
        column = (x + offset) % X
        return Slab(lambda at, zs: gathered.at[at, column, zs, 3:6], y_lo, at_y, 42 + 4 * offset)

    slabs = [(slab_x(offset), slab_y(offset)) for offset in range(4)]

    def each(action, *offsets):
        for offset in offsets:
            for slab in slabs[offset]:
                action(slab)

    cz = Ring(lambda at, h: gathered.at[2 * h : 2 * h + 2, :, at, 6:9], z, at_z, 12, Z, 4)

    @pl.loop(1, Z)
    def _(i):
        z_in(i).wait_recv()

    ay.begin()
    bx.begin()
    each(Slab.begin, 0)

    @pl.loop(1, TP)
    def _(i):
        t_in(i).wait_recv()

    cz.begin()
    ay.land(1, 0)
    bx.land(1, 0)
    ay.land(1, 1)
    bx.land(1, 1)
    each(Slab.begin, 3, 1)
    cz.land(1, 0)
    ay.land(2, 0)
    bx.land(2, 0)
    each(Slab.begin, 2)
    cz.land(1, 1)
    each(Slab.land, 0)
    cz.land(2, 0)
    each(Slab.land, 3)
    cz.land(2, 1)
    each(Slab.land, 1)
    cz.land(3, 0)
    each(Slab.land, 2)
    query_copy.wait_recv()
    each(Slab.finish, 0, 3, 1)
    cz.land(3, 1)
    cz.land(4, 0)
    each(Slab.finish, 2)

    page_of = lax.broadcasted_iota(jnp.int32, (256, HEADS), 0) // 16
    blank = jnp.zeros((ROPE, HEADS), jnp.bfloat16)

    def prefix(query, p):
        limit = pages[p]
        latent, rotary = query[:LAT], query[LAT:]
        keys = [
            jnp.concatenate(
                [gathered[:, :, 2 * lanes + tokens, p].reshape(256, 128) for lanes in range(4)], axis=1
            )
            for tokens in range(2)
        ]
        packed = gathered[:, :, p, PROMPTS].reshape(256, 128)
        scores = []
        for tokens in range(2):
            parts = [rotary, blank] if tokens == 0 else [blank, rotary]
            score = lax.dot_general(keys[tokens], latent, NN, preferred_element_type=jnp.float32)
            score = score + lax.dot_general(
                packed, jnp.concatenate(parts, axis=0), NN, preferred_element_type=jnp.float32
            )
            scores.append(jnp.where(page_of < limit, score * SCALE, BIG_NEGATIVE))
        return attend(scores, [lambda key=key: key for key in keys])

    returns = []
    for row in range(ROWS_DEV):
        peak, total, numerator = prefix(others[row], other_prompt[row])
        partial[row, :, :LAT] = numerator
        partial[row, :, LAT : LAT + 128] = peak
        partial[row, :, LAT + 128 :] = total
        back = remote(partial.at[row], arrived.at[row], c_send.at[2 + row], c_recv.at[2 + row], twin)
        back.start()
        returns.append(back)

    for row in range(ROWS_DEV):
        peak, total, numerator = prefix(queries[row], prompt[row])
        returns[row].wait_recv()
        m0, t0 = stats[row, 0], stats[row, 1]
        m1, t1 = arrived[row, :, LAT : LAT + 128], arrived[row, :, LAT + 128 :]
        top = jnp.maximum(jnp.maximum(peak, m0), m1)
        f, f0, f1 = jnp.exp(peak - top), jnp.exp(m0 - top), jnp.exp(m1 - top)
        whole = total * f + t0 * f0 + t1 * f1
        f, f0, f1 = f / whole, f0 / whole, f1 / whole
        for lanes in range(0, LAT, 128):
            part = slice(lanes, lanes + 128)
            summed = numerator[:, part] * f + numer[row, :, part] * f0 + arrived[row, :, part] * f1
            out[row, :, part] = summed.astype(out.dtype)

    @pl.loop(1, NEAR)
    def _(i):
        spread(i).wait_send()

    @pl.loop(1, Z)
    def _(i):
        z_out(i).wait_send()

    @pl.loop(1, TP)
    def _(i):
        t_out(i).wait_send()

    for copy in started + [trade, prompt_copy, query_copy] + returns:
        copy.wait_send()


def on_device(
    q_latent, page_pool, block_table, cache_len, prompt_of_row, prefix_cache, prefix_pages, owners
):
    anywhere = pl.BlockSpec(memory_space=pl.ANY)
    i32 = jnp.int32
    bf16, f32 = jnp.bfloat16, jnp.float32
    dma = pltpu.SemaphoreType.DMA
    return pl.pallas_call(
        kernel,
        out_shape=jax.ShapeDtypeStruct((ROWS_DEV, HEADS, LAT), bf16),
        in_specs=[anywhere] * 8,
        out_specs=pl.BlockSpec(memory_space=pltpu.VMEM),
        scratch_shapes=[
            pltpu.SMEM((ROWS_DEV, MAXP), i32),
            pltpu.SMEM((ROWS_DEV,), i32),
            pltpu.SMEM((ROWS_DEV,), i32),
            pltpu.SMEM((PROMPTS,), i32),
            pltpu.SMEM((PROMPTS,), i32),
            pltpu.VMEM((ROWS_DEV, WIDTH, HEADS), bf16),
            pltpu.VMEM((1, PAGE, WIDTH), bf16),
            pltpu.VMEM((Y, X, Z, POS, 16, 128), bf16),
            pltpu.VMEM((NEAR, 2, 16, 128), bf16),
            pltpu.VMEM((POS, 16, 128), bf16),
            pltpu.VMEM((POS, 16, 128), bf16),
            pltpu.VMEM((2, Z, 2, 16, 128), bf16),
            pltpu.VMEM((ROWS_DEV * MAXP, PAGE, WIDTH), bf16),
            pltpu.VMEM((ROWS_DEV, WIDTH, HEADS), bf16),
            pltpu.VMEM((ROWS_DEV,), i32),
            pltpu.SMEM((ROWS_DEV,), i32),
            pltpu.VMEM((ROWS_DEV, HEADS, LAT + 256), f32),
            pltpu.VMEM((ROWS_DEV, HEADS, LAT + 256), f32),
            pltpu.VMEM((ROWS_DEV, HEADS, LAT), f32),
            pltpu.VMEM((ROWS_DEV, 2, HEADS, 128), f32),
            dma((8,)), dma,
            dma((NEAR,)), dma((NEAR,)),
            dma((Z,)), dma((Z,)),
            dma((TP,)), dma((TP,)),
            dma((58,)), dma((58,)),
            dma((5,)), dma((5,)),
        ],
        compiler_params=pltpu.CompilerParams(
            collective_id=0, has_side_effects=True, vmem_limit_bytes=60 * 1024 * 1024
        ),
        cost_estimate=pl.CostEstimate(flops=1200000000, bytes_accessed=3000000, transcendentals=600000),
    )(
        block_table, cache_len, prompt_of_row, prefix_pages, owners,
        jnp.swapaxes(q_latent, 1, 2), prefix_cache, page_pool,
    )


def solution(mesh):
    placed = (
        P(("dp", "tp"), None, None),
        P(("dp", "tp"), None, None),
        P(("dp", "tp"), None),
        P(("dp", "tp")),
        P(("dp", "tp")),
        P("dp", "tp", None),
        P(),
        P(),
    )
    return jax.shard_map(
        on_device,
        mesh=mesh,
        in_specs=placed,
        out_specs=P(("dp", "tp"), None, None),
        check_vma=False,
    )
```

```python
import jax
import jax.numpy as jnp
from jax import lax
from jax.experimental import pallas as pl
from jax.experimental.pallas import tpu as pltpu
from jax.sharding import PartitionSpec as P

LAT = 512
ROPE = 64
WIDTH = LAT + ROPE
HEADS = 128
PAGE = 64
MAXP = 16
PROMPTS = 8
ROWS_DEV = 2
X, Y, Z, DP, TP = 4, 4, 8, 32, 16
NEAR = 2 * Z
POS = PROMPTS + 1
SCALE = 192.0 ** (-0.5)
BIG_NEGATIVE = -1e30
MESH = pl.DeviceIdType.MESH
TN = (((0,), (0,)), ((), ()))
NN = (((1,), (0,)), ((), ()))


def kernel(
    table_hbm, length_hbm, prompt_hbm, pages_hbm, owners_hbm, queries_hbm, slot_hbm, pool_hbm, out,
    table, length, prompt, pages, owners, queries, slot, gathered, received, picked, traded, staged, pool, others, other_block,
    other_prompt, partial, arrived, numer, stats,
    local_sem, prompt_sem, p1_send, p1_recv, z_send, z_recv, t_send, t_recv, r_send, r_recv, c_send, c_recv,
):
    dp = lax.axis_index("dp")
    tp = lax.axis_index("tp")
    core = dp % 2
    z = (dp // 2) % Z
    y_hi = dp // (2 * Z)
    y_lo = tp // X
    x = tp % X
    twin = (dp + 1 - 2 * core, tp)

    def at_y(step):
        y = (y_hi * Y + y_lo + step + 2 * Y) % (2 * Y)
        return (((y // Y) * Z + z) * 2 + core, (y % Y) * X + x)

    def at_x(step):
        return (dp, y_lo * X + (x + step + X) % X)

    def at_z(step):
        return ((y_hi * Z + (z + step + Z) % Z) * 2 + core, tp)

    barrier = pltpu.get_barrier_semaphore()

    def near(i):
        return y_hi * NEAR + (dp + i) % NEAR

    partner = ((1 - y_hi) * NEAR + dp % NEAR, tp)

    @pl.loop(1, NEAR)
    def _(i):
        pl.semaphore_signal(barrier, inc=1, device_id=(near(i), tp), device_id_type=MESH)

    pl.semaphore_signal(barrier, inc=1, device_id=partner, device_id_type=MESH)

    @pl.loop(1, TP)
    def _(i):
        pl.semaphore_signal(barrier, inc=1, device_id=(dp, (tp + i) % TP), device_id_type=MESH)

    for step in (1, -1):
        pl.semaphore_signal(barrier, inc=1, device_id=at_y(step), device_id_type=MESH)

    slot_copy, query_in, pool_copy, *small_copies = [
        pltpu.make_async_copy(source, target, local_sem.at[i])
        for i, (source, target) in enumerate((
            (slot_hbm, slot), (queries_hbm, queries), (pool_hbm, pool), (owners_hbm, owners),
            (prompt_hbm, prompt), (pages_hbm, pages), (table_hbm, table), (length_hbm, length),
        ))
    ]
    for copy in [slot_copy, query_in, pool_copy] + small_copies:
        copy.start()

    slot_copy.wait()

    for half in range(2):
        low = slot[0, 32 * half : 32 * half + 16, LAT:WIDTH]
        high = slot[0, 32 * half + 16 : 32 * half + 32, LAT:WIDTH]
        rotary = jnp.concatenate([low, high], axis=1)
        for tile in range(Z):
            lanes, tokens = tile // 2, tile % 2
            first = 32 * half + 16 * tokens
            staged[half, tile, 0] = slot[0, first : first + 16, 128 * lanes : 128 * lanes + 128]
            staged[half, tile, 1] = rotary

    pl.semaphore_wait(barrier, NEAR - 1 + 1 + TP - 1 + 2)

    def remote(src, dst, send, recv, device):
        return pltpu.make_async_remote_copy(
            src_ref=src, dst_ref=dst, send_sem=send, recv_sem=recv, device_id=device, device_id_type=MESH
        )

    def spread(i):
        to = near(i)
        return remote(
            staged.at[to % 2, (to // 2) % Z], received.at[dp % NEAR], p1_send.at[i], p1_recv.at[i], (to, tp)
        )

    def spread_in(i):
        source = (dp - i + DP) % NEAR
        return remote(
            staged.at[0, 0], received.at[source], p1_send.at[i], p1_recv.at[i], (near(i), tp)
        )

    @pl.loop(1, NEAR)
    def _(i):
        spread(i).start()

    received[dp % NEAR] = staged[core, z]
    prompt_copy = remote(prompt_hbm, other_block, c_send.at[0], c_recv.at[0], twin)
    prompt_copy.start()
    query_copy = remote(queries_hbm, others, c_send.at[1], c_recv.at[1], twin)
    query_copy.start()
    for copy in [query_in] + small_copies:
        copy.wait()

    token = lax.broadcasted_iota(jnp.int32, (MAXP * PAGE, HEADS), 0)

    def turned_wide(line):
        return jnp.transpose(jnp.broadcast_to(line, (HEADS, HEADS)))

    def attend(score, values):
        peak = jnp.max(score, axis=0, keepdims=True)
        weight = jnp.exp(score - peak)
        total = jnp.sum(weight, axis=0, keepdims=True)
        numerator = lax.dot_general(
            weight.astype(jnp.bfloat16), values, TN, preferred_element_type=jnp.float32
        )
        return turned_wide(peak), turned_wide(total), numerator

    def private(row):
        keys = jnp.concatenate([pool[table[row, i]] for i in range(MAXP)], axis=0)
        score = lax.dot_general(keys, queries[row], NN, preferred_element_type=jnp.float32)
        score = jnp.where(token < length[row], score * SCALE, BIG_NEGATIVE)
        peak, total, numerator = attend(score, keys[:, :LAT])
        numer[row] = numerator
        stats[row, 0] = peak
        stats[row, 1] = total

    pool_copy.wait()
    private(0)

    @pl.loop(1, NEAR)
    def _(i):
        spread_in(i).wait_recv()

    for p in range(PROMPTS):
        picked[p] = received[owners[p] % NEAR, 0]
    picked[PROMPTS] = received[owners[z] % NEAR, 1]
    trade = remote(picked, traded, c_send.at[4], c_recv.at[4], partner)
    trade.start()
    trade.wait_recv()
    for p in range(POS):
        owner = owners[p] if p < PROMPTS else owners[z]
        gathered[y_lo, x, z, p] = jnp.where(owner // NEAR == y_hi, picked[p], traded[p])

    def z_out(i):
        mine = gathered.at[y_lo, x, z, 0:6]
        return remote(mine, mine, z_send.at[i], z_recv.at[i], at_z(i))

    def z_in(i):
        theirs = gathered.at[y_lo, x, (z - i + Z) % Z, 0:6]
        return remote(theirs, theirs, z_send.at[i], z_recv.at[i], at_z(i))

    def t_out(i):
        mine = gathered.at[y_lo, x, z, 6:9]
        return remote(mine, mine, t_send.at[i], t_recv.at[i], (dp, (tp + i) % TP))

    def t_in(i):
        source = (tp - i + TP) % TP
        theirs = gathered.at[source // X, source % X, z, 6:9]
        return remote(theirs, theirs, t_send.at[i], t_recv.at[i], (dp, (tp + i) % TP))

    @pl.loop(1, Z)
    def _(i):
        z_out(i).start()

    @pl.loop(1, TP)
    def _(i):
        t_out(i).start()

    private(1)
    prompt_copy.wait_recv()
    to_scalar = pltpu.make_async_copy(other_block, other_prompt, prompt_sem)
    to_scalar.start()
    to_scalar.wait()

    started = []

    class Ring:
        def __init__(self, half, place, device, first, size, steps):
            self.half, self.place, self.device = half, place, device
            self.first, self.size, self.steps = first, size, steps

        def copy(self, step, number, way, behind):
            sign = 1 - 2 * way
            origin = (self.place - sign * behind + 2 * self.size) % self.size
            ref = self.half(origin, number if way == 0 else 1 - number)
            index = self.first + 2 * (2 * (step - 1) + number) + way
            return remote(ref, ref, r_send.at[index], r_recv.at[index], self.device(sign))

        def send(self, step, number):
            for way in range(2):
                copy = self.copy(step, number, way, step - 1)
                copy.start()
                started.append(copy)

        def begin(self):
            self.send(1, 0)
            self.send(1, 1)

        def land(self, step, number):
            forward = step + 1 < self.steps or (step + 1 == self.steps and number == 0)
            for way in range(2):
                self.copy(step, number, way, step).wait_recv()
                if forward:
                    copy = self.copy(step + 1, number, way, step)
                    copy.start()
                    started.append(copy)

    ay = Ring(lambda y, h: gathered.at[y, x, 4 * h : 4 * h + 4, 0:3], y_lo, at_y, 0, Y, 2)
    bx = Ring(lambda at, h: gathered.at[y_lo, at, 4 * h : 4 * h + 4, 3:6], x, at_x, 6, X, 2)
    class Slab:
        def __init__(self, piece, place, device, first):
            self.piece, self.place, self.device, self.first = piece, place, device, first

        def copy(self, step, way, behind):
            sign = 1 - 2 * way
            origin = (self.place - sign * behind + 8) % 4
            ref = self.piece(origin, pl.ds(0, Z) if step == 1 else pl.ds(4 * way, 4))
            index = self.first + 2 * (step - 1) + way
            return remote(ref, ref, r_send.at[index], r_recv.at[index], self.device(sign))

        def begin(self):
            for way in range(2):
                copy = self.copy(1, way, 0)
                copy.start()
                started.append(copy)

        def land(self):
            for way in range(2):
                self.copy(1, way, 1).wait_recv()
                copy = self.copy(2, way, 1)
                copy.start()
                started.append(copy)

        def finish(self):
            for way in range(2):
                self.copy(2, way, 2).wait_recv()

    def slab_x(offset):
        row = (y_lo + offset) % Y
        return Slab(lambda at, zs: gathered.at[row, at, zs, 0:3], x, at_x, 26 + 4 * offset)

    def slab_y(offset):
        column = (x + offset) % X
        return Slab(lambda at, zs: gathered.at[at, column, zs, 3:6], y_lo, at_y, 42 + 4 * offset)

    slabs = [(slab_x(offset), slab_y(offset)) for offset in range(4)]

    def each(action, *offsets):
        for offset in offsets:
            for slab in slabs[offset]:
                action(slab)

    cz = Ring(lambda at, h: gathered.at[2 * h : 2 * h + 2, :, at, 6:9], z, at_z, 12, Z, 4)

    @pl.loop(1, Z)
    def _(i):
        z_in(i).wait_recv()

    ay.begin()
    bx.begin()
    each(Slab.begin, 0)

    @pl.loop(1, TP)
    def _(i):
        t_in(i).wait_recv()

    cz.begin()
    ay.land(1, 0)
    bx.land(1, 0)
    ay.land(1, 1)
    bx.land(1, 1)
    each(Slab.begin, 3, 1)
    cz.land(1, 0)
    ay.land(2, 0)
    bx.land(2, 0)
    each(Slab.begin, 2)
    cz.land(1, 1)
    each(Slab.land, 0)
    cz.land(2, 0)
    each(Slab.land, 3)
    cz.land(2, 1)
    each(Slab.land, 1)
    cz.land(3, 0)
    each(Slab.land, 2)
    query_copy.wait_recv()
    each(Slab.finish, 0, 3, 1)
    cz.land(3, 1)
    cz.land(4, 0)
    each(Slab.finish, 2)

    page_of = lax.broadcasted_iota(jnp.int32, (512, HEADS), 0) // 16 % TP
    blank = jnp.zeros((ROPE, HEADS), jnp.bfloat16)

    def prefix(query, p):
        latent, rotary = query[:LAT], query[LAT:]
        keys = jnp.concatenate(
            [
                jnp.concatenate(
                    [gathered[:, :, 2 * lanes + tokens, p].reshape(256, 128) for lanes in range(4)], axis=1
                )
                for tokens in range(2)
            ],
            axis=0,
        )
        packed = gathered[:, :, p, PROMPTS].reshape(256, 128)
        turned = [
            lax.dot_general(
                packed, jnp.concatenate(parts, axis=0), NN, preferred_element_type=jnp.float32
            )
            for parts in ([rotary, blank], [blank, rotary])
        ]
        score = lax.dot_general(keys, latent, NN, preferred_element_type=jnp.float32)
        score = (score + jnp.concatenate(turned, axis=0)) * SCALE
        return attend(jnp.where(page_of < pages[p], score, BIG_NEGATIVE), keys)

    returns = []
    for row in range(ROWS_DEV):
        peak, total, numerator = prefix(others[row], other_prompt[row])
        partial[row, :, :LAT] = numerator
        partial[row, :, LAT : LAT + 128] = peak
        partial[row, :, LAT + 128 :] = total
        back = remote(partial.at[row], arrived.at[row], c_send.at[2 + row], c_recv.at[2 + row], twin)
        back.start()
        returns.append(back)

    for row in range(ROWS_DEV):
        peak, total, numerator = prefix(queries[row], prompt[row])
        returns[row].wait_recv()
        m0, t0 = stats[row, 0], stats[row, 1]
        m1, t1 = arrived[row, :, LAT : LAT + 128], arrived[row, :, LAT + 128 :]
        top = jnp.maximum(jnp.maximum(peak, m0), m1)
        f, f0, f1 = jnp.exp(peak - top), jnp.exp(m0 - top), jnp.exp(m1 - top)
        whole = total * f + t0 * f0 + t1 * f1
        f, f0, f1 = f / whole, f0 / whole, f1 / whole
        for lanes in range(0, LAT, 128):
            part = slice(lanes, lanes + 128)
            summed = numerator[:, part] * f + numer[row, :, part] * f0 + arrived[row, :, part] * f1
            out[row, :, part] = summed.astype(out.dtype)

    @pl.loop(1, NEAR)
    def _(i):
        spread(i).wait_send()

    @pl.loop(1, Z)
    def _(i):
        z_out(i).wait_send()

    @pl.loop(1, TP)
    def _(i):
        t_out(i).wait_send()

    for copy in started + [trade, prompt_copy, query_copy] + returns:
        copy.wait_send()


def on_device(
    q_latent, page_pool, block_table, cache_len, prompt_of_row, prefix_cache, prefix_pages, owners
):
    anywhere = pl.BlockSpec(memory_space=pl.ANY)
    i32 = jnp.int32
    bf16, f32 = jnp.bfloat16, jnp.float32
    dma = pltpu.SemaphoreType.DMA
    return pl.pallas_call(
        kernel,
        out_shape=jax.ShapeDtypeStruct((ROWS_DEV, HEADS, LAT), bf16),
        in_specs=[anywhere] * 8,
        out_specs=pl.BlockSpec(memory_space=pltpu.VMEM),
        scratch_shapes=[
            pltpu.SMEM((ROWS_DEV, MAXP), i32),
            pltpu.SMEM((ROWS_DEV,), i32),
            pltpu.SMEM((ROWS_DEV,), i32),
            pltpu.SMEM((PROMPTS,), i32),
            pltpu.SMEM((PROMPTS,), i32),
            pltpu.VMEM((ROWS_DEV, WIDTH, HEADS), bf16),
            pltpu.VMEM((1, PAGE, WIDTH), bf16),
            pltpu.VMEM((Y, X, Z, POS, 16, 128), bf16),
            pltpu.VMEM((NEAR, 2, 16, 128), bf16),
            pltpu.VMEM((POS, 16, 128), bf16),
            pltpu.VMEM((POS, 16, 128), bf16),
            pltpu.VMEM((2, Z, 2, 16, 128), bf16),
            pltpu.VMEM((ROWS_DEV * MAXP, PAGE, WIDTH), bf16),
            pltpu.VMEM((ROWS_DEV, WIDTH, HEADS), bf16),
            pltpu.VMEM((ROWS_DEV,), i32),
            pltpu.SMEM((ROWS_DEV,), i32),
            pltpu.VMEM((ROWS_DEV, HEADS, LAT + 256), f32),
            pltpu.VMEM((ROWS_DEV, HEADS, LAT + 256), f32),
            pltpu.VMEM((ROWS_DEV, HEADS, LAT), f32),
            pltpu.VMEM((ROWS_DEV, 2, HEADS, 128), f32),
            dma((8,)), dma,
            dma((NEAR,)), dma((NEAR,)),
            dma((Z,)), dma((Z,)),
            dma((TP,)), dma((TP,)),
            dma((58,)), dma((58,)),
            dma((5,)), dma((5,)),
        ],
        compiler_params=pltpu.CompilerParams(
            collective_id=0, has_side_effects=True, vmem_limit_bytes=60 * 1024 * 1024
        ),
        cost_estimate=pl.CostEstimate(flops=1200000000, bytes_accessed=3000000, transcendentals=600000),
    )(
        block_table, cache_len, prompt_of_row, prefix_pages, owners,
        jnp.swapaxes(q_latent, 1, 2), prefix_cache, page_pool,
    )


def solution(mesh):
    placed = (
        P(("dp", "tp"), None, None),
        P(("dp", "tp"), None, None),
        P(("dp", "tp"), None),
        P(("dp", "tp")),
        P(("dp", "tp")),
        P("dp", "tp", None),
        P(),
        P(),
    )
    return jax.shard_map(
        on_device,
        mesh=mesh,
        in_specs=placed,
        out_specs=P(("dp", "tp"), None, None),
        check_vma=False,
    )
```

```python
import jax
import jax.numpy as jnp
from jax import lax
from jax.experimental import pallas as pl
from jax.experimental.pallas import tpu as pltpu
from jax.sharding import PartitionSpec as P

LAT = 512
ROPE = 64
WIDTH = LAT + ROPE
HEADS = 128
PAGE = 64
MAXP = 16
PROMPTS = 8
ROWS_DEV = 2
X, Y, Z, DP, TP = 4, 4, 8, 32, 16
NEAR = 2 * Z
POS = PROMPTS + 1
SCALE = 192.0 ** (-0.5)
BIG_NEGATIVE = -1e30
MESH = pl.DeviceIdType.MESH
TN = (((0,), (0,)), ((), ()))
NN = (((1,), (0,)), ((), ()))


def kernel(
    table_hbm, length_hbm, prompt_hbm, pages_hbm, owners_hbm, queries_hbm, slot_hbm, pool_hbm, out,
    table, length, prompt, pages, owners, queries, slot, gathered, received, picked, traded, staged, pool, others, other_block,
    other_prompt, partial, arrived, numer, stats,
    local_sem, prompt_sem, p1_send, p1_recv, z_send, z_recv, t_send, t_recv, r_send, r_recv, c_send, c_recv,
):
    dp = lax.axis_index("dp")
    tp = lax.axis_index("tp")
    core = dp % 2
    z = (dp // 2) % Z
    y_hi = dp // (2 * Z)
    y_lo = tp // X
    x = tp % X
    twin = (dp + 1 - 2 * core, tp)

    def at_y(step):
        y = (y_hi * Y + y_lo + step + 2 * Y) % (2 * Y)
        return (((y // Y) * Z + z) * 2 + core, (y % Y) * X + x)

    def at_x(step):
        return (dp, y_lo * X + (x + step + X) % X)

    def at_z(step):
        return ((y_hi * Z + (z + step + Z) % Z) * 2 + core, tp)

    barrier = pltpu.get_barrier_semaphore()

    def near(i):
        return y_hi * NEAR + (dp + i) % NEAR

    partner = ((1 - y_hi) * NEAR + dp % NEAR, tp)

    @pl.loop(1, NEAR)
    def _(i):
        pl.semaphore_signal(barrier, inc=1, device_id=(near(i), tp), device_id_type=MESH)

    pl.semaphore_signal(barrier, inc=1, device_id=partner, device_id_type=MESH)

    for step in (1, -1):
        pl.semaphore_signal(barrier, inc=1, device_id=at_x(step), device_id_type=MESH)
    for step in (1, -1, 2, -2):
        pl.semaphore_signal(barrier, inc=1, device_id=at_y(step), device_id_type=MESH)

    slot_copy, query_in, pool_copy, *small_copies = [
        pltpu.make_async_copy(source, target, local_sem.at[i])
        for i, (source, target) in enumerate((
            (slot_hbm, slot), (queries_hbm, queries), (pool_hbm, pool), (owners_hbm, owners),
            (prompt_hbm, prompt), (pages_hbm, pages), (table_hbm, table), (length_hbm, length),
        ))
    ]
    for copy in [slot_copy, query_in, pool_copy] + small_copies:
        copy.start()

    slot_copy.wait()

    for half in range(2):
        low = slot[0, 32 * half : 32 * half + 16, LAT:WIDTH]
        high = slot[0, 32 * half + 16 : 32 * half + 32, LAT:WIDTH]
        rotary = jnp.concatenate([low, high], axis=1)
        for tile in range(Z):
            lanes, tokens = tile // 2, tile % 2
            first = 32 * half + 16 * tokens
            staged[half, tile, 0] = slot[0, first : first + 16, 128 * lanes : 128 * lanes + 128]
            staged[half, tile, 1] = rotary

    pl.semaphore_wait(barrier, NEAR - 1 + 1 + 2 + 4)

    def remote(src, dst, send, recv, device):
        return pltpu.make_async_remote_copy(
            src_ref=src, dst_ref=dst, send_sem=send, recv_sem=recv, device_id=device, device_id_type=MESH
        )

    def spread(i):
        to = near(i)
        return remote(
            staged.at[to % 2, (to // 2) % Z], received.at[dp % NEAR], p1_send.at[i], p1_recv.at[i], (to, tp)
        )

    def spread_in(i):
        source = (dp - i + DP) % NEAR
        return remote(
            staged.at[0, 0], received.at[source], p1_send.at[i], p1_recv.at[i], (near(i), tp)
        )

    @pl.loop(1, NEAR)
    def _(i):
        spread(i).start()

    received[dp % NEAR] = staged[core, z]
    prompt_copy = remote(prompt_hbm, other_block, c_send.at[0], c_recv.at[0], twin)
    prompt_copy.start()
    query_copy = remote(queries_hbm, others, c_send.at[1], c_recv.at[1], twin)
    query_copy.start()
    for copy in [query_in] + small_copies:
        copy.wait()

    token = lax.broadcasted_iota(jnp.int32, (MAXP * PAGE, HEADS), 0)

    def turned_wide(line):
        return jnp.transpose(jnp.broadcast_to(line, (HEADS, HEADS)))

    def attend(score, values):
        peak = jnp.max(score, axis=0, keepdims=True)
        weight = jnp.exp(score - peak)
        total = jnp.sum(weight, axis=0, keepdims=True)
        numerator = lax.dot_general(
            weight.astype(jnp.bfloat16), values, TN, preferred_element_type=jnp.float32
        )
        return turned_wide(peak), turned_wide(total), numerator

    def private(row):
        keys = jnp.concatenate([pool[table[row, i]] for i in range(MAXP)], axis=0)
        score = lax.dot_general(keys, queries[row], NN, preferred_element_type=jnp.float32)
        score = jnp.where(token < length[row], score * SCALE, BIG_NEGATIVE)
        peak, total, numerator = attend(score, keys[:, :LAT])
        numer[row] = numerator
        stats[row, 0] = peak
        stats[row, 1] = total

    pool_copy.wait()
    private(0)
    prompt_copy.wait_recv()
    to_scalar = pltpu.make_async_copy(other_block, other_prompt, prompt_sem)
    to_scalar.start()

    @pl.loop(1, NEAR)
    def _(i):
        spread_in(i).wait_recv()

    for p in range(PROMPTS):
        picked[p] = received[owners[p] % NEAR, 0]
    picked[PROMPTS] = received[owners[z] % NEAR, 1]
    trade = remote(picked, traded, c_send.at[4], c_recv.at[4], partner)
    trade.start()
    private(1)
    trade.wait_recv()
    for p in range(POS):
        owner = owners[p] if p < PROMPTS else owners[z]
        gathered[y_lo, x, z, p] = jnp.where(owner // NEAR == y_hi, picked[p], traded[p])

    z_moves = (
        (1, 0, 0, 6), (-1, 0, 0, 6), (2, 0, 0, 6), (-2, 0, 0, 6),
        (2, -1, 0, 6), (-2, 1, 0, 6), (2, -2, 0, 3), (-2, 2, 3, 6),
    )

    def z_copy(number, arriving):
        to, origin, low, high = z_moves[number]
        at = (z + origin - (to if arriving else 0) + 2 * Z) % Z
        ref = gathered.at[y_lo, x, at, low:high]
        return remote(ref, ref, z_send.at[number], z_recv.at[number], at_z(to))

    y_moves = ((1, 6, 9), (-1, 6, 9), (2, 6, 8), (-2, 8, 9))

    def y_copy(number, arriving):
        to, low, high = y_moves[number]
        at = (y_lo - (to if arriving else 0) + Y) % Y
        ref = gathered.at[at, x, z, low:high]
        return remote(ref, ref, t_send.at[number], t_recv.at[number], at_y(to))

    for number in range(4):
        y_copy(number, False).start()
        z_copy(number, False).start()

    started = []

    class Ring:
        def __init__(self, half, place, device, first, size, steps):
            self.half, self.place, self.device = half, place, device
            self.first, self.size, self.steps = first, size, steps

        def copy(self, step, number, way, behind):
            sign = 1 - 2 * way
            origin = (self.place - sign * behind + 2 * self.size) % self.size
            ref = self.half(origin, number if way == 0 else 1 - number)
            index = self.first + 2 * (2 * (step - 1) + number) + way
            return remote(ref, ref, r_send.at[index], r_recv.at[index], self.device(sign))

        def send(self, step, number):
            for way in range(2):
                copy = self.copy(step, number, way, step - 1)
                copy.start()
                started.append(copy)

        def begin(self):
            self.send(1, 0)
            self.send(1, 1)

        def land(self, step, number):
            forward = step + 1 < self.steps or (step + 1 == self.steps and number == 0)
            for way in range(2):
                self.copy(step, number, way, step).wait_recv()
                if forward:
                    copy = self.copy(step + 1, number, way, step)
                    copy.start()
                    started.append(copy)

    ay = Ring(lambda y, h: gathered.at[y, x, 4 * h : 4 * h + 4, 0:3], y_lo, at_y, 0, Y, 2)
    bx = Ring(lambda at, h: gathered.at[y_lo, at, 4 * h : 4 * h + 4, 3:6], x, at_x, 6, X, 2)
    class Slab:
        def __init__(self, piece, place, device, first):
            self.piece, self.place, self.device, self.first = piece, place, device, first

        def copy(self, step, way, behind):
            sign = 1 - 2 * way
            origin = (self.place - sign * behind + 8) % 4
            ref = self.piece(origin, pl.ds(0, Z) if step == 1 else pl.ds(4 * way, 4))
            index = self.first + 2 * (step - 1) + way
            return remote(ref, ref, r_send.at[index], r_recv.at[index], self.device(sign))

        def begin(self):
            for way in range(2):
                copy = self.copy(1, way, 0)
                copy.start()
                started.append(copy)

        def land(self):
            for way in range(2):
                self.copy(1, way, 1).wait_recv()
                copy = self.copy(2, way, 1)
                copy.start()
                started.append(copy)

        def finish(self):
            for way in range(2):
                self.copy(2, way, 2).wait_recv()

    def slab_x(offset):
        row = (y_lo + offset) % Y
        return Slab(lambda at, zs: gathered.at[row, at, zs, 0:3], x, at_x, 26 + 4 * offset)

    def slab_y(offset):
        column = (x + offset) % X
        return Slab(lambda at, zs: gathered.at[at, column, zs, 3:6], y_lo, at_y, 42 + 4 * offset)

    slabs = [(slab_x(offset), slab_y(offset)) for offset in range(4)]

    def each(action, *offsets):
        for offset in offsets:
            for slab in slabs[offset]:
                action(slab)

    cz = Ring(lambda at, h: gathered.at[2 * h : 2 * h + 2, :, at, 6:9], z, at_z, 12, Z, 4)
    cx = Ring(lambda at, h: gathered.at[2 * h : 2 * h + 2, at, z, 6:9], x, at_x, 58, X, 2)

    for number in range(4):
        y_copy(number, True).wait_recv()
    cx.begin()
    for number in range(4):
        z_copy(number, True).wait_recv()
        z_copy(number + 4, False).start()
    cx.land(1, 0)
    cx.land(1, 1)
    cx.land(2, 0)
    cz.begin()
    for number in range(4, 8):
        z_copy(number, True).wait_recv()
    ay.begin()
    bx.begin()
    each(Slab.begin, 0)

    ay.land(1, 0)
    bx.land(1, 0)
    ay.land(1, 1)
    bx.land(1, 1)
    each(Slab.begin, 3, 1)
    cz.land(1, 0)
    ay.land(2, 0)
    bx.land(2, 0)
    each(Slab.begin, 2)
    cz.land(1, 1)
    each(Slab.land, 0)
    cz.land(2, 0)
    each(Slab.land, 3)
    cz.land(2, 1)
    each(Slab.land, 1)
    cz.land(3, 0)
    each(Slab.land, 2)
    query_copy.wait_recv()
    each(Slab.finish, 0, 3, 1)
    cz.land(3, 1)
    cz.land(4, 0)
    each(Slab.finish, 2)

    page_of = lax.broadcasted_iota(jnp.int32, (512, HEADS), 0) // 16 % TP
    blank = jnp.zeros((ROPE, HEADS), jnp.bfloat16)

    def prefix(query, p):
        latent, rotary = query[:LAT], query[LAT:]
        keys = jnp.concatenate(
            [
                jnp.concatenate(
                    [gathered[:, :, 2 * lanes + tokens, p].reshape(256, 128) for lanes in range(4)], axis=1
                )
                for tokens in range(2)
            ],
            axis=0,
        )
        packed = gathered[:, :, p, PROMPTS].reshape(256, 128)
        turned = [
            lax.dot_general(
                packed, jnp.concatenate(parts, axis=0), NN, preferred_element_type=jnp.float32
            )
            for parts in ([rotary, blank], [blank, rotary])
        ]
        score = lax.dot_general(keys, latent, NN, preferred_element_type=jnp.float32)
        score = (score + jnp.concatenate(turned, axis=0)) * SCALE
        return attend(jnp.where(page_of < pages[p], score, BIG_NEGATIVE), keys)

    to_scalar.wait()
    returns = []
    for row in range(ROWS_DEV):
        peak, total, numerator = prefix(others[row], other_prompt[row])
        partial[row, :, :LAT] = numerator
        partial[row, :, LAT : LAT + 128] = peak
        partial[row, :, LAT + 128 :] = total
        back = remote(partial.at[row], arrived.at[row], c_send.at[2 + row], c_recv.at[2 + row], twin)
        back.start()
        returns.append(back)

    for row in range(ROWS_DEV):
        peak, total, numerator = prefix(queries[row], prompt[row])
        returns[row].wait_recv()
        m0, t0 = stats[row, 0], stats[row, 1]
        m1, t1 = arrived[row, :, LAT : LAT + 128], arrived[row, :, LAT + 128 :]
        top = jnp.maximum(jnp.maximum(peak, m0), m1)
        f, f0, f1 = jnp.exp(peak - top), jnp.exp(m0 - top), jnp.exp(m1 - top)
        whole = total * f + t0 * f0 + t1 * f1
        f, f0, f1 = f / whole, f0 / whole, f1 / whole
        for lanes in range(0, LAT, 128):
            part = slice(lanes, lanes + 128)
            summed = numerator[:, part] * f + numer[row, :, part] * f0 + arrived[row, :, part] * f1
            out[row, :, part] = summed.astype(out.dtype)

    @pl.loop(1, NEAR)
    def _(i):
        spread(i).wait_send()

    for number in range(8):
        z_copy(number, False).wait_send()
    for number in range(4):
        y_copy(number, False).wait_send()
    for copy in started + [trade, prompt_copy, query_copy] + returns:
        copy.wait_send()


def on_device(
    q_latent, page_pool, block_table, cache_len, prompt_of_row, prefix_cache, prefix_pages, owners
):
    anywhere = pl.BlockSpec(memory_space=pl.ANY)
    i32 = jnp.int32
    bf16, f32 = jnp.bfloat16, jnp.float32
    dma = pltpu.SemaphoreType.DMA
    return pl.pallas_call(
        kernel,
        out_shape=jax.ShapeDtypeStruct((ROWS_DEV, HEADS, LAT), bf16),
        in_specs=[anywhere] * 8,
        out_specs=pl.BlockSpec(memory_space=pltpu.VMEM),
        scratch_shapes=[
            pltpu.SMEM((ROWS_DEV, MAXP), i32),
            pltpu.SMEM((ROWS_DEV,), i32),
            pltpu.SMEM((ROWS_DEV,), i32),
            pltpu.SMEM((PROMPTS,), i32),
            pltpu.SMEM((PROMPTS,), i32),
            pltpu.VMEM((ROWS_DEV, WIDTH, HEADS), bf16),
            pltpu.VMEM((1, PAGE, WIDTH), bf16),
            pltpu.VMEM((Y, X, Z, POS, 16, 128), bf16),
            pltpu.VMEM((NEAR, 2, 16, 128), bf16),
            pltpu.VMEM((POS, 16, 128), bf16),
            pltpu.VMEM((POS, 16, 128), bf16),
            pltpu.VMEM((2, Z, 2, 16, 128), bf16),
            pltpu.VMEM((ROWS_DEV * MAXP, PAGE, WIDTH), bf16),
            pltpu.VMEM((ROWS_DEV, WIDTH, HEADS), bf16),
            pltpu.VMEM((ROWS_DEV,), i32),
            pltpu.SMEM((ROWS_DEV,), i32),
            pltpu.VMEM((ROWS_DEV, HEADS, LAT + 256), f32),
            pltpu.VMEM((ROWS_DEV, HEADS, LAT + 256), f32),
            pltpu.VMEM((ROWS_DEV, HEADS, LAT), f32),
            pltpu.VMEM((ROWS_DEV, 2, HEADS, 128), f32),
            dma((8,)), dma,
            dma((NEAR,)), dma((NEAR,)),
            dma((Z,)), dma((Z,)),
            dma((4,)), dma((4,)),
            dma((64,)), dma((64,)),
            dma((5,)), dma((5,)),
        ],
        compiler_params=pltpu.CompilerParams(
            collective_id=0, has_side_effects=True, vmem_limit_bytes=60 * 1024 * 1024
        ),
        cost_estimate=pl.CostEstimate(flops=1200000000, bytes_accessed=3000000, transcendentals=600000),
    )(
        block_table, cache_len, prompt_of_row, prefix_pages, owners,
        jnp.swapaxes(q_latent, 1, 2), prefix_cache, page_pool,
    )


def solution(mesh):
    placed = (
        P(("dp", "tp"), None, None),
        P(("dp", "tp"), None, None),
        P(("dp", "tp"), None),
        P(("dp", "tp")),
        P(("dp", "tp")),
        P("dp", "tp", None),
        P(),
        P(),
    )
    return jax.shard_map(
        on_device,
        mesh=mesh,
        in_specs=placed,
        out_specs=P(("dp", "tp"), None, None),
        check_vma=False,
    )
```

```python
import jax
import jax.numpy as jnp
from jax import lax
from jax.experimental import pallas as pl
from jax.experimental.pallas import tpu as pltpu
from jax.sharding import PartitionSpec as P

LAT = 512
ROPE = 64
WIDTH = LAT + ROPE
HEADS = 128
PAGE = 64
MAXP = 16
PROMPTS = 8
ROWS_DEV = 2
X, Y, Z, DP, TP = 4, 4, 8, 32, 16
NEAR = 2 * Z
POS = PROMPTS + 1
SCALE = 192.0 ** (-0.5)
BIG_NEGATIVE = -1e30
MESH = pl.DeviceIdType.MESH
TN = (((0,), (0,)), ((), ()))
NN = (((1,), (0,)), ((), ()))


def each_of(first, end):
    def run(body):
        for i in range(first, end):
            body(i)

    return run


def kernel(
    table_hbm, length_hbm, prompt_hbm, pages_hbm, owners_hbm, queries_hbm, slot_hbm, pool_hbm, out,
    table, length, prompt, pages, owners, queries, slot, gathered, received, picked, traded, staged, pool, others, other_block,
    other_prompt, partial, arrived, numer, stats,
    local_sem, prompt_sem, p1_send, p1_recv, z_send, z_recv, t_send, t_recv, r_send, r_recv, c_send, c_recv,
):
    dp = lax.axis_index("dp")
    tp = lax.axis_index("tp")
    core = dp % 2
    z = (dp // 2) % Z
    y_hi = dp // (2 * Z)
    y_lo = tp // X
    x = tp % X
    twin = (dp + 1 - 2 * core, tp)

    def at_y(step):
        y = (y_hi * Y + y_lo + step + 2 * Y) % (2 * Y)
        return (((y // Y) * Z + z) * 2 + core, (y % Y) * X + x)

    def at_x(step):
        return (dp, y_lo * X + (x + step + X) % X)

    def at_z(step):
        return ((y_hi * Z + (z + step + Z) % Z) * 2 + core, tp)

    barrier = pltpu.get_barrier_semaphore()

    def near(i):
        return y_hi * NEAR + (dp + i) % NEAR

    partner = ((1 - y_hi) * NEAR + dp % NEAR, tp)

    @each_of(1, NEAR)
    def _(i):
        pl.semaphore_signal(barrier, inc=1, device_id=(near(i), tp), device_id_type=MESH)

    pl.semaphore_signal(barrier, inc=1, device_id=partner, device_id_type=MESH)

    @each_of(1, TP)
    def _(i):
        pl.semaphore_signal(barrier, inc=1, device_id=(dp, (tp + i) % TP), device_id_type=MESH)

    for step in (1, -1):
        pl.semaphore_signal(barrier, inc=1, device_id=at_y(step), device_id_type=MESH)

    slot_copy, query_in, pool_copy, *small_copies = [
        pltpu.make_async_copy(source, target, local_sem.at[i])
        for i, (source, target) in enumerate((
            (slot_hbm, slot), (queries_hbm, queries), (pool_hbm, pool), (owners_hbm, owners),
            (prompt_hbm, prompt), (pages_hbm, pages), (table_hbm, table), (length_hbm, length),
        ))
    ]
    for copy in [slot_copy, query_in, pool_copy] + small_copies:
        copy.start()

    slot_copy.wait()

    for half in range(2):
        low = slot[0, 32 * half : 32 * half + 16, LAT:WIDTH]
        high = slot[0, 32 * half + 16 : 32 * half + 32, LAT:WIDTH]
        rotary = jnp.concatenate([low, high], axis=1)
        for tile in range(Z):
            lanes, tokens = tile // 2, tile % 2
            first = 32 * half + 16 * tokens
            staged[half, tile, 0] = slot[0, first : first + 16, 128 * lanes : 128 * lanes + 128]
            staged[half, tile, 1] = rotary

    pl.semaphore_wait(barrier, NEAR - 1 + 1 + TP - 1 + 2)

    def remote(src, dst, send, recv, device):
        return pltpu.make_async_remote_copy(
            src_ref=src, dst_ref=dst, send_sem=send, recv_sem=recv, device_id=device, device_id_type=MESH
        )

    def spread(i):
        to = near(i)
        return remote(
            staged.at[to % 2, (to // 2) % Z], received.at[dp % NEAR], p1_send.at[i], p1_recv.at[i], (to, tp)
        )

    def spread_in(i):
        source = (dp - i + DP) % NEAR
        return remote(
            staged.at[0, 0], received.at[source], p1_send.at[i], p1_recv.at[i], (near(i), tp)
        )

    @each_of(1, NEAR)
    def _(i):
        spread(i).start()

    received[dp % NEAR] = staged[core, z]
    prompt_copy = remote(prompt_hbm, other_block, c_send.at[0], c_recv.at[0], twin)
    prompt_copy.start()
    query_copy = remote(queries_hbm, others, c_send.at[1], c_recv.at[1], twin)
    query_copy.start()
    for copy in [query_in] + small_copies:
        copy.wait()

    token = lax.broadcasted_iota(jnp.int32, (MAXP * PAGE, HEADS), 0)

    def turned_wide(line):
        return jnp.transpose(jnp.broadcast_to(line, (HEADS, HEADS)))

    def attend(score, values):
        peak = jnp.max(score, axis=0, keepdims=True)
        weight = jnp.exp(score - peak)
        total = jnp.sum(weight, axis=0, keepdims=True)
        numerator = lax.dot_general(
            weight.astype(jnp.bfloat16), values, TN, preferred_element_type=jnp.float32
        )
        return turned_wide(peak), turned_wide(total), numerator

    def private(row):
        keys = jnp.concatenate([pool[table[row, i]] for i in range(MAXP)], axis=0)
        score = lax.dot_general(keys, queries[row], NN, preferred_element_type=jnp.float32)
        score = jnp.where(token < length[row], score * SCALE, BIG_NEGATIVE)
        peak, total, numerator = attend(score, keys[:, :LAT])
        numer[row] = numerator
        stats[row, 0] = peak
        stats[row, 1] = total

    pool_copy.wait()
    private(0)
    prompt_copy.wait_recv()
    to_scalar = pltpu.make_async_copy(other_block, other_prompt, prompt_sem)
    to_scalar.start()

    @each_of(1, NEAR)
    def _(i):
        spread_in(i).wait_recv()

    for p in range(PROMPTS):
        picked[p] = received[owners[p] % NEAR, 0]
    picked[PROMPTS] = received[owners[z] % NEAR, 1]
    trade = remote(picked, traded, c_send.at[4], c_recv.at[4], partner)
    trade.start()
    trade.wait_recv()
    for p in range(POS):
        owner = owners[p] if p < PROMPTS else owners[z]
        gathered[y_lo, x, z, p] = jnp.where(owner // NEAR == y_hi, picked[p], traded[p])

    def z_out(i):
        mine = gathered.at[y_lo, x, z, 0:6]
        return remote(mine, mine, z_send.at[i], z_recv.at[i], at_z(i))

    def z_in(i):
        theirs = gathered.at[y_lo, x, (z - i + Z) % Z, 0:6]
        return remote(theirs, theirs, z_send.at[i], z_recv.at[i], at_z(i))

    def t_out(i):
        mine = gathered.at[y_lo, x, z, 6:9]
        return remote(mine, mine, t_send.at[i], t_recv.at[i], (dp, (tp + i) % TP))

    def t_in(i):
        source = (tp - i + TP) % TP
        theirs = gathered.at[source // X, source % X, z, 6:9]
        return remote(theirs, theirs, t_send.at[i], t_recv.at[i], (dp, (tp + i) % TP))

    @each_of(1, Z)
    def _(i):
        z_out(i).start()

    @each_of(1, TP)
    def _(i):
        t_out(i).start()

    private(1)
    started = []

    class Ring:
        def __init__(self, half, place, device, first, size, steps):
            self.half, self.place, self.device = half, place, device
            self.first, self.size, self.steps = first, size, steps

        def copy(self, step, number, way, behind):
            sign = 1 - 2 * way
            origin = (self.place - sign * behind + 2 * self.size) % self.size
            ref = self.half(origin, number if way == 0 else 1 - number)
            index = self.first + 2 * (2 * (step - 1) + number) + way
            return remote(ref, ref, r_send.at[index], r_recv.at[index], self.device(sign))

        def send(self, step, number):
            for way in range(2):
                copy = self.copy(step, number, way, step - 1)
                copy.start()
                started.append(copy)

        def begin(self):
            self.send(1, 0)
            self.send(1, 1)

        def land(self, step, number):
            forward = step + 1 < self.steps or (step + 1 == self.steps and number == 0)
            for way in range(2):
                self.copy(step, number, way, step).wait_recv()
                if forward:
                    copy = self.copy(step + 1, number, way, step)
                    copy.start()
                    started.append(copy)

    ay = Ring(lambda y, h: gathered.at[y, x, 4 * h : 4 * h + 4, 0:3], y_lo, at_y, 0, Y, 2)
    bx = Ring(lambda at, h: gathered.at[y_lo, at, 4 * h : 4 * h + 4, 3:6], x, at_x, 6, X, 2)
    class Slab:
        def __init__(self, piece, place, device, first):
            self.piece, self.place, self.device, self.first = piece, place, device, first

        def copy(self, step, way, behind):
            sign = 1 - 2 * way
            origin = (self.place - sign * behind + 8) % 4
            ref = self.piece(origin, pl.ds(0, Z) if step == 1 else pl.ds(4 * way, 4))
            index = self.first + 2 * (step - 1) + way
            return remote(ref, ref, r_send.at[index], r_recv.at[index], self.device(sign))

        def begin(self):
            for way in range(2):
                copy = self.copy(1, way, 0)
                copy.start()
                started.append(copy)

        def land(self):
            for way in range(2):
                self.copy(1, way, 1).wait_recv()
                copy = self.copy(2, way, 1)
                copy.start()
                started.append(copy)

        def finish(self):
            for way in range(2):
                self.copy(2, way, 2).wait_recv()

    def slab_x(offset):
        row = (y_lo + offset) % Y
        return Slab(lambda at, zs: gathered.at[row, at, zs, 0:3], x, at_x, 26 + 4 * offset)

    def slab_y(offset):
        column = (x + offset) % X
        return Slab(lambda at, zs: gathered.at[at, column, zs, 3:6], y_lo, at_y, 42 + 4 * offset)

    slabs = [(slab_x(offset), slab_y(offset)) for offset in range(4)]

    def each(action, *offsets):
        for offset in offsets:
            for slab in slabs[offset]:
                action(slab)

    cz = Ring(lambda at, h: gathered.at[2 * h : 2 * h + 2, :, at, 6:9], z, at_z, 12, Z, 4)

    @each_of(1, Z)
    def _(i):
        z_in(i).wait_recv()

    ay.begin()
    bx.begin()
    each(Slab.begin, 0)

    @each_of(1, TP)
    def _(i):
        t_in(i).wait_recv()

    cz.begin()
    ay.land(1, 0)
    bx.land(1, 0)
    ay.land(1, 1)
    bx.land(1, 1)
    each(Slab.begin, 3, 1)
    cz.land(1, 0)
    ay.land(2, 0)
    bx.land(2, 0)
    each(Slab.begin, 2)
    cz.land(1, 1)
    each(Slab.land, 0)
    cz.land(2, 0)
    each(Slab.land, 3)
    cz.land(2, 1)
    each(Slab.land, 1)
    cz.land(3, 0)
    each(Slab.land, 2)
    query_copy.wait_recv()
    each(Slab.finish, 0, 3, 1)
    cz.land(3, 1)
    cz.land(4, 0)
    each(Slab.finish, 2)

    page_of = lax.broadcasted_iota(jnp.int32, (512, HEADS), 0) // 16 % TP
    blank = jnp.zeros((ROPE, HEADS), jnp.bfloat16)

    def prefix(query, p):
        latent, rotary = query[:LAT], query[LAT:]
        keys = jnp.concatenate(
            [
                jnp.concatenate(
                    [gathered[:, :, 2 * lanes + tokens, p].reshape(256, 128) for lanes in range(4)], axis=1
                )
                for tokens in range(2)
            ],
            axis=0,
        )
        packed = gathered[:, :, p, PROMPTS].reshape(256, 128)
        turned = [
            lax.dot_general(
                packed, jnp.concatenate(parts, axis=0), NN, preferred_element_type=jnp.float32
            )
            for parts in ([rotary, blank], [blank, rotary])
        ]
        score = lax.dot_general(keys, latent, NN, preferred_element_type=jnp.float32)
        score = (score + jnp.concatenate(turned, axis=0)) * SCALE
        return attend(jnp.where(page_of < pages[p], score, BIG_NEGATIVE), keys)

    to_scalar.wait()
    returns = []
    for row in range(ROWS_DEV):
        peak, total, numerator = prefix(others[row], other_prompt[row])
        partial[row, :, :LAT] = numerator
        partial[row, :, LAT : LAT + 128] = peak
        partial[row, :, LAT + 128 :] = total
        back = remote(partial.at[row], arrived.at[row], c_send.at[2 + row], c_recv.at[2 + row], twin)
        back.start()
        returns.append(back)

    for row in range(ROWS_DEV):
        peak, total, numerator = prefix(queries[row], prompt[row])
        returns[row].wait_recv()
        m0, t0 = stats[row, 0], stats[row, 1]
        m1, t1 = arrived[row, :, LAT : LAT + 128], arrived[row, :, LAT + 128 :]
        top = jnp.maximum(jnp.maximum(peak, m0), m1)
        f, f0, f1 = jnp.exp(peak - top), jnp.exp(m0 - top), jnp.exp(m1 - top)
        whole = total * f + t0 * f0 + t1 * f1
        f, f0, f1 = f / whole, f0 / whole, f1 / whole
        for lanes in range(0, LAT, 128):
            part = slice(lanes, lanes + 128)
            summed = numerator[:, part] * f + numer[row, :, part] * f0 + arrived[row, :, part] * f1
            out[row, :, part] = summed.astype(out.dtype)

    @each_of(1, NEAR)
    def _(i):
        spread(i).wait_send()

    @each_of(1, Z)
    def _(i):
        z_out(i).wait_send()

    @each_of(1, TP)
    def _(i):
        t_out(i).wait_send()

    for copy in started + [trade, prompt_copy, query_copy] + returns:
        copy.wait_send()


def on_device(
    q_latent, page_pool, block_table, cache_len, prompt_of_row, prefix_cache, prefix_pages, owners
):
    anywhere = pl.BlockSpec(memory_space=pl.ANY)
    i32 = jnp.int32
    bf16, f32 = jnp.bfloat16, jnp.float32
    dma = pltpu.SemaphoreType.DMA
    return pl.pallas_call(
        kernel,
        out_shape=jax.ShapeDtypeStruct((ROWS_DEV, HEADS, LAT), bf16),
        in_specs=[anywhere] * 8,
        out_specs=pl.BlockSpec(memory_space=pltpu.VMEM),
        scratch_shapes=[
            pltpu.SMEM((ROWS_DEV, MAXP), i32),
            pltpu.SMEM((ROWS_DEV,), i32),
            pltpu.SMEM((ROWS_DEV,), i32),
            pltpu.SMEM((PROMPTS,), i32),
            pltpu.SMEM((PROMPTS,), i32),
            pltpu.VMEM((ROWS_DEV, WIDTH, HEADS), bf16),
            pltpu.VMEM((1, PAGE, WIDTH), bf16),
            pltpu.VMEM((Y, X, Z, POS, 16, 128), bf16),
            pltpu.VMEM((NEAR, 2, 16, 128), bf16),
            pltpu.VMEM((POS, 16, 128), bf16),
            pltpu.VMEM((POS, 16, 128), bf16),
            pltpu.VMEM((2, Z, 2, 16, 128), bf16),
            pltpu.VMEM((ROWS_DEV * MAXP, PAGE, WIDTH), bf16),
            pltpu.VMEM((ROWS_DEV, WIDTH, HEADS), bf16),
            pltpu.VMEM((ROWS_DEV,), i32),
            pltpu.SMEM((ROWS_DEV,), i32),
            pltpu.VMEM((ROWS_DEV, HEADS, LAT + 256), f32),
            pltpu.VMEM((ROWS_DEV, HEADS, LAT + 256), f32),
            pltpu.VMEM((ROWS_DEV, HEADS, LAT), f32),
            pltpu.VMEM((ROWS_DEV, 2, HEADS, 128), f32),
            dma((8,)), dma,
            dma((NEAR,)), dma((NEAR,)),
            dma((Z,)), dma((Z,)),
            dma((TP,)), dma((TP,)),
            dma((58,)), dma((58,)),
            dma((5,)), dma((5,)),
        ],
        compiler_params=pltpu.CompilerParams(
            collective_id=0, has_side_effects=True, vmem_limit_bytes=60 * 1024 * 1024
        ),
        cost_estimate=pl.CostEstimate(flops=1200000000, bytes_accessed=3000000, transcendentals=600000),
    )(
        block_table, cache_len, prompt_of_row, prefix_pages, owners,
        jnp.swapaxes(q_latent, 1, 2), prefix_cache, page_pool,
    )


def solution(mesh):
    placed = (
        P(("dp", "tp"), None, None),
        P(("dp", "tp"), None, None),
        P(("dp", "tp"), None),
        P(("dp", "tp")),
        P(("dp", "tp")),
        P("dp", "tp", None),
        P(),
        P(),
    )
    return jax.shard_map(
        on_device,
        mesh=mesh,
        in_specs=placed,
        out_specs=P(("dp", "tp"), None, None),
        check_vma=False,
    )
```

```python
import jax
import jax.numpy as jnp
from jax import lax
from jax.experimental import pallas as pl
from jax.experimental.pallas import tpu as pltpu
from jax.sharding import PartitionSpec as P

LAT = 512
ROPE = 64
WIDTH = LAT + ROPE
HEADS = 128
PAGE = 64
MAXP = 16
PROMPTS = 8
ROWS_DEV = 2
X, Y, Z, DP, TP = 4, 4, 8, 32, 16
NEAR = 2 * Z
NEAR_ORDER = sorted(range(1, NEAR), key=lambda i: -min(i, NEAR - i))
Z_ORDER = sorted(range(1, Z), key=lambda i: -min(i, Z - i))
TP_ORDER = [4 * dy + dx for dx in (2, 1, 3, 0) for dy in (2, 1, 3, 0)][:-1]
POS = PROMPTS + 1
SCALE = 192.0 ** (-0.5)
BIG_NEGATIVE = -1e30
MESH = pl.DeviceIdType.MESH
TN = (((0,), (0,)), ((), ()))
NN = (((1,), (0,)), ((), ()))


def each_of(numbers):
    def run(body):
        for i in numbers:
            body(i)

    return run


def kernel(
    table_hbm, length_hbm, prompt_hbm, pages_hbm, owners_hbm, queries_hbm, slot_hbm, pool_hbm, out_hbm,
    table, length, prompt, pages, owners, queries, slot, gathered, received, picked, traded, staged, pool, others, other_block,
    other_prompt, partial, arrived, numer, stats, out,
    local_sem, prompt_sem, p1_send, p1_recv, z_send, z_recv, t_send, t_recv, r_send, r_recv, c_send, c_recv,
):
    dp = lax.axis_index("dp")
    tp = lax.axis_index("tp")
    core = dp % 2
    z = (dp // 2) % Z
    y_hi = dp // (2 * Z)
    y_lo = tp // X
    x = tp % X
    twin = (dp + 1 - 2 * core, tp)

    def at_y(step):
        y = (y_hi * Y + y_lo + step + 2 * Y) % (2 * Y)
        return (((y // Y) * Z + z) * 2 + core, (y % Y) * X + x)

    def at_x(step):
        return (dp, y_lo * X + (x + step + X) % X)

    def at_z(step):
        return ((y_hi * Z + (z + step + Z) % Z) * 2 + core, tp)

    barrier = pltpu.get_barrier_semaphore()

    def near(i):
        return y_hi * NEAR + (dp + i) % NEAR

    def group(i, sign):
        return (y_lo + sign * (i // X) + Y) % Y * X + (x + sign * (i % X) + X) % X

    partner = ((1 - y_hi) * NEAR + dp % NEAR, tp)

    @each_of(NEAR_ORDER)
    def _(i):
        pl.semaphore_signal(barrier, inc=1, device_id=(near(i), tp), device_id_type=MESH)

    pl.semaphore_signal(barrier, inc=1, device_id=partner, device_id_type=MESH)

    @each_of(TP_ORDER)
    def _(i):
        pl.semaphore_signal(barrier, inc=1, device_id=(dp, group(i, 1)), device_id_type=MESH)

    for step in (1, -1):
        pl.semaphore_signal(barrier, inc=1, device_id=at_y(step), device_id_type=MESH)

    slot_copy, query_in, pool_copy, *small_copies = [
        pltpu.make_async_copy(source, target, local_sem.at[i])
        for i, (source, target) in enumerate((
            (slot_hbm, slot), (queries_hbm, queries), (pool_hbm, pool), (owners_hbm, owners),
            (prompt_hbm, prompt), (pages_hbm, pages), (table_hbm, table), (length_hbm, length),
        ))
    ]
    for copy in [slot_copy, query_in, pool_copy] + small_copies:
        copy.start()

    slot_copy.wait()

    for half in range(2):
        low = slot[0, 32 * half : 32 * half + 16, LAT:WIDTH]
        high = slot[0, 32 * half + 16 : 32 * half + 32, LAT:WIDTH]
        rotary = jnp.concatenate([low, high], axis=1)
        for tile in range(Z):
            lanes, tokens = tile // 2, tile % 2
            first = 32 * half + 16 * tokens
            staged[half, tile, 0] = slot[0, first : first + 16, 128 * lanes : 128 * lanes + 128]
            staged[half, tile, 1] = rotary

    pl.semaphore_wait(barrier, NEAR - 1 + 1 + TP - 1 + 2)

    def remote(src, dst, send, recv, device):
        return pltpu.make_async_remote_copy(
            src_ref=src, dst_ref=dst, send_sem=send, recv_sem=recv, device_id=device, device_id_type=MESH
        )

    def spread(i):
        to = near(i)
        return remote(
            staged.at[to % 2, (to // 2) % Z], received.at[dp % NEAR], p1_send.at[i], p1_recv.at[i], (to, tp)
        )

    def spread_in(i):
        source = (dp - i + DP) % NEAR
        return remote(
            staged.at[0, 0], received.at[source], p1_send.at[i], p1_recv.at[i], (near(i), tp)
        )

    @each_of(NEAR_ORDER)
    def _(i):
        spread(i).start()

    received[dp % NEAR] = staged[core, z]
    prompt_copy = remote(prompt_hbm, other_block, c_send.at[0], c_recv.at[0], twin)
    prompt_copy.start()
    query_copy = remote(queries_hbm, others, c_send.at[1], c_recv.at[1], twin)
    query_copy.start()
    for copy in [query_in] + small_copies:
        copy.wait()

    token = lax.broadcasted_iota(jnp.int32, (MAXP * PAGE, HEADS), 0)

    def turned_wide(line):
        return jnp.transpose(jnp.broadcast_to(line, (HEADS, HEADS)))

    def attend(score, values):
        peak = jnp.max(score, axis=0, keepdims=True)
        weight = jnp.exp(score - peak)
        total = jnp.sum(weight, axis=0, keepdims=True)
        numerator = lax.dot_general(
            weight.astype(jnp.bfloat16), values, TN, preferred_element_type=jnp.float32
        )
        return turned_wide(peak), turned_wide(total), numerator

    def private(row):
        keys = jnp.concatenate([pool[table[row, i]] for i in range(MAXP)], axis=0)
        score = lax.dot_general(keys, queries[row], NN, preferred_element_type=jnp.float32)
        score = jnp.where(token < length[row], score * SCALE, BIG_NEGATIVE)
        peak, total, numerator = attend(score, keys[:, :LAT])
        numer[row] = numerator
        stats[row, 0] = peak
        stats[row, 1] = total

    pool_copy.wait()
    private(0)
    prompt_copy.wait_recv()
    to_scalar = pltpu.make_async_copy(other_block, other_prompt, prompt_sem)
    to_scalar.start()

    @each_of(NEAR_ORDER)
    def _(i):
        spread_in(i).wait_recv()

    for p in range(PROMPTS):
        picked[p] = received[owners[p] % NEAR, 0]
    picked[PROMPTS] = received[owners[z] % NEAR, 1]
    trade = remote(picked, traded, c_send.at[4], c_recv.at[4], partner)
    trade.start()
    trade.wait_recv()
    for p in range(POS):
        owner = owners[p] if p < PROMPTS else owners[z]
        gathered[y_lo, x, z, p] = jnp.where(owner // NEAR == y_hi, picked[p], traded[p])

    def z_out(i):
        mine = gathered.at[y_lo, x, z, 0:6]
        return remote(mine, mine, z_send.at[i], z_recv.at[i], at_z(i))

    def z_in(i):
        theirs = gathered.at[y_lo, x, (z - i + Z) % Z, 0:6]
        return remote(theirs, theirs, z_send.at[i], z_recv.at[i], at_z(i))

    def t_out(i):
        mine = gathered.at[y_lo, x, z, 6:9]
        return remote(mine, mine, t_send.at[i], t_recv.at[i], (dp, group(i, 1)))

    def t_in(i):
        source = group(i, -1)
        theirs = gathered.at[source // X, source % X, z, 6:9]
        return remote(theirs, theirs, t_send.at[i], t_recv.at[i], (dp, group(i, 1)))

    @each_of(Z_ORDER)
    def _(i):
        z_out(i).start()

    @each_of(TP_ORDER)
    def _(i):
        t_out(i).start()

    private(1)
    started = []

    class Ring:
        def __init__(self, half, place, device, first, size, steps):
            self.half, self.place, self.device = half, place, device
            self.first, self.size, self.steps = first, size, steps

        def copy(self, step, number, way, behind):
            sign = 1 - 2 * way
            origin = (self.place - sign * behind + 2 * self.size) % self.size
            ref = self.half(origin, number if way == 0 else 1 - number)
            index = self.first + 2 * (2 * (step - 1) + number) + way
            return remote(ref, ref, r_send.at[index], r_recv.at[index], self.device(sign))

        def send(self, step, number):
            for way in range(2):
                copy = self.copy(step, number, way, step - 1)
                copy.start()
                started.append(copy)

        def begin(self):
            self.send(1, 0)
            self.send(1, 1)

        def land(self, step, number):
            forward = step + 1 < self.steps or (step + 1 == self.steps and number == 0)
            for way in range(2):
                self.copy(step, number, way, step).wait_recv()
                if forward:
                    copy = self.copy(step + 1, number, way, step)
                    copy.start()
                    started.append(copy)

    ay = Ring(lambda y, h: gathered.at[y, x, 4 * h : 4 * h + 4, 0:3], y_lo, at_y, 0, Y, 2)
    bx = Ring(lambda at, h: gathered.at[y_lo, at, 4 * h : 4 * h + 4, 3:6], x, at_x, 6, X, 2)
    class Slab:
        def __init__(self, piece, place, device, first):
            self.piece, self.place, self.device, self.first = piece, place, device, first

        def copy(self, step, way, behind):
            sign = 1 - 2 * way
            origin = (self.place - sign * behind + 8) % 4
            ref = self.piece(origin, pl.ds(0, Z) if step == 1 else pl.ds(4 * way, 4))
            index = self.first + 2 * (step - 1) + way
            return remote(ref, ref, r_send.at[index], r_recv.at[index], self.device(sign))

        def begin(self):
            for way in range(2):
                copy = self.copy(1, way, 0)
                copy.start()
                started.append(copy)

        def land(self):
            for way in range(2):
                self.copy(1, way, 1).wait_recv()
                copy = self.copy(2, way, 1)
                copy.start()
                started.append(copy)

        def finish(self):
            for way in range(2):
                self.copy(2, way, 2).wait_recv()

    def slab_x(offset):
        row = (y_lo + offset) % Y
        return Slab(lambda at, zs: gathered.at[row, at, zs, 0:3], x, at_x, 26 + 4 * offset)

    def slab_y(offset):
        column = (x + offset) % X
        return Slab(lambda at, zs: gathered.at[at, column, zs, 3:6], y_lo, at_y, 42 + 4 * offset)

    slabs = [(slab_x(offset), slab_y(offset)) for offset in range(4)]

    def each(action, *offsets):
        for offset in offsets:
            for slab in slabs[offset]:
                action(slab)

    cz = Ring(lambda at, h: gathered.at[2 * h : 2 * h + 2, :, at, 6:9], z, at_z, 12, Z, 4)

    @each_of(Z_ORDER)
    def _(i):
        z_in(i).wait_recv()

    ay.begin()
    bx.begin()
    each(Slab.begin, 0)

    @each_of(TP_ORDER)
    def _(i):
        t_in(i).wait_recv()

    cz.begin()
    ay.land(1, 0)
    bx.land(1, 0)
    ay.land(1, 1)
    bx.land(1, 1)
    each(Slab.begin, 3, 1)
    cz.land(1, 0)
    ay.land(2, 0)
    bx.land(2, 0)
    each(Slab.begin, 2)
    cz.land(1, 1)
    each(Slab.land, 0)
    cz.land(2, 0)
    each(Slab.land, 3)
    cz.land(2, 1)
    each(Slab.land, 1)
    cz.land(3, 0)
    each(Slab.land, 2)
    query_copy.wait_recv()
    each(Slab.finish, 0, 3, 1)
    cz.land(3, 1)
    cz.land(4, 0)
    each(Slab.finish, 2)

    page_of = lax.broadcasted_iota(jnp.int32, (512, HEADS), 0) // 16 % TP
    blank = jnp.zeros((ROPE, HEADS), jnp.bfloat16)

    def prefix(query, p):
        latent, rotary = query[:LAT], query[LAT:]
        keys = jnp.concatenate(
            [
                jnp.concatenate(
                    [gathered[:, :, 2 * lanes + tokens, p].reshape(256, 128) for lanes in range(4)], axis=1
                )
                for tokens in range(2)
            ],
            axis=0,
        )
        packed = gathered[:, :, p, PROMPTS].reshape(256, 128)
        turned = [
            lax.dot_general(
                packed, jnp.concatenate(parts, axis=0), NN, preferred_element_type=jnp.float32
            )
            for parts in ([rotary, blank], [blank, rotary])
        ]
        score = lax.dot_general(keys, latent, NN, preferred_element_type=jnp.float32)
        score = (score + jnp.concatenate(turned, axis=0)) * SCALE
        return attend(jnp.where(page_of < pages[p], score, BIG_NEGATIVE), keys)

    to_scalar.wait()
    returns = []
    results = []
    for row in range(ROWS_DEV):
        peak, total, numerator = prefix(others[row], other_prompt[row])
        partial[row, :, :LAT] = numerator
        partial[row, :, LAT : LAT + 128] = peak
        partial[row, :, LAT + 128 :] = total
        back = remote(partial.at[row], arrived.at[row], c_send.at[2 + row], c_recv.at[2 + row], twin)
        back.start()
        returns.append(back)

    for row in range(ROWS_DEV):
        peak, total, numerator = prefix(queries[row], prompt[row])
        returns[row].wait_recv()
        m0, t0 = stats[row, 0], stats[row, 1]
        m1, t1 = arrived[row, :, LAT : LAT + 128], arrived[row, :, LAT + 128 :]
        top = jnp.maximum(jnp.maximum(peak, m0), m1)
        f, f0, f1 = jnp.exp(peak - top), jnp.exp(m0 - top), jnp.exp(m1 - top)
        whole = total * f + t0 * f0 + t1 * f1
        f, f0, f1 = f / whole, f0 / whole, f1 / whole
        for lanes in range(0, LAT, 128):
            part = slice(lanes, lanes + 128)
            summed = numerator[:, part] * f + numer[row, :, part] * f0 + arrived[row, :, part] * f1
            out[row, :, part] = summed.astype(out.dtype)
        result = pltpu.make_async_copy(out.at[row], out_hbm.at[row], local_sem.at[8 + row])
        result.start()
        results.append(result)

    @each_of(NEAR_ORDER)
    def _(i):
        spread(i).wait_send()

    @each_of(Z_ORDER)
    def _(i):
        z_out(i).wait_send()

    @each_of(TP_ORDER)
    def _(i):
        t_out(i).wait_send()

    for copy in started + [trade, prompt_copy, query_copy] + returns:
        copy.wait_send()
    for result in results:
        result.wait()


def on_device(
    q_latent, page_pool, block_table, cache_len, prompt_of_row, prefix_cache, prefix_pages, owners
):
    anywhere = pl.BlockSpec(memory_space=pl.ANY)
    i32 = jnp.int32
    bf16, f32 = jnp.bfloat16, jnp.float32
    dma = pltpu.SemaphoreType.DMA
    return pl.pallas_call(
        kernel,
        out_shape=jax.ShapeDtypeStruct((ROWS_DEV, HEADS, LAT), bf16),
        in_specs=[anywhere] * 8,
        out_specs=anywhere,
        scratch_shapes=[
            pltpu.SMEM((ROWS_DEV, MAXP), i32),
            pltpu.SMEM((ROWS_DEV,), i32),
            pltpu.SMEM((ROWS_DEV,), i32),
            pltpu.SMEM((PROMPTS,), i32),
            pltpu.SMEM((PROMPTS,), i32),
            pltpu.VMEM((ROWS_DEV, WIDTH, HEADS), bf16),
            pltpu.VMEM((1, PAGE, WIDTH), bf16),
            pltpu.VMEM((Y, X, Z, POS, 16, 128), bf16),
            pltpu.VMEM((NEAR, 2, 16, 128), bf16),
            pltpu.VMEM((POS, 16, 128), bf16),
            pltpu.VMEM((POS, 16, 128), bf16),
            pltpu.VMEM((2, Z, 2, 16, 128), bf16),
            pltpu.VMEM((ROWS_DEV * MAXP, PAGE, WIDTH), bf16),
            pltpu.VMEM((ROWS_DEV, WIDTH, HEADS), bf16),
            pltpu.VMEM((ROWS_DEV,), i32),
            pltpu.SMEM((ROWS_DEV,), i32),
            pltpu.VMEM((ROWS_DEV, HEADS, LAT + 256), f32),
            pltpu.VMEM((ROWS_DEV, HEADS, LAT + 256), f32),
            pltpu.VMEM((ROWS_DEV, HEADS, LAT), f32),
            pltpu.VMEM((ROWS_DEV, 2, HEADS, 128), f32),
            pltpu.VMEM((ROWS_DEV, HEADS, LAT), bf16),
            dma((10,)), dma,
            dma((NEAR,)), dma((NEAR,)),
            dma((Z,)), dma((Z,)),
            dma((TP,)), dma((TP,)),
            dma((58,)), dma((58,)),
            dma((5,)), dma((5,)),
        ],
        compiler_params=pltpu.CompilerParams(
            collective_id=0, has_side_effects=True, vmem_limit_bytes=60 * 1024 * 1024
        ),
        cost_estimate=pl.CostEstimate(flops=1200000000, bytes_accessed=3000000, transcendentals=600000),
    )(
        block_table, cache_len, prompt_of_row, prefix_pages, owners,
        jnp.swapaxes(q_latent, 1, 2), prefix_cache, page_pool,
    )


def solution(mesh):
    placed = (
        P(("dp", "tp"), None, None),
        P(("dp", "tp"), None, None),
        P(("dp", "tp"), None),
        P(("dp", "tp")),
        P(("dp", "tp")),
        P("dp", "tp", None),
        P(),
        P(),
    )
    return jax.shard_map(
        on_device,
        mesh=mesh,
        in_specs=placed,
        out_specs=P(("dp", "tp"), None, None),
        check_vma=False,
    )
```

```python
import jax
import jax.numpy as jnp
from jax import lax
from jax.experimental import pallas as pl
from jax.experimental.pallas import tpu as pltpu
from jax.sharding import PartitionSpec as P

LAT = 512
ROPE = 64
WIDTH = LAT + ROPE
HEADS = 128
PAGE = 64
MAXP = 16
PROMPTS = 8
ROWS_DEV = 2
X, Y, Z, DP, TP = 4, 4, 8, 32, 16
NEAR = 2 * Z
NEAR_ORDER = sorted(range(1, NEAR), key=lambda i: -min(i, NEAR - i))
Z_ORDER = sorted(range(1, Z), key=lambda i: -min(i, Z - i))
TP_ORDER = [4 * dy + dx for dx in (2, 1, 3, 0) for dy in (2, 1, 3, 0)][:-1]
POS = PROMPTS + 1
SCALE = 192.0 ** (-0.5)
BIG_NEGATIVE = -1e30
MESH = pl.DeviceIdType.MESH
TN = (((0,), (0,)), ((), ()))
NN = (((1,), (0,)), ((), ()))


def each_of(numbers):
    def run(body):
        for i in numbers:
            body(i)

    return run


def kernel(
    table_hbm, length_hbm, prompt_hbm, pages_hbm, owners_hbm, queries_hbm, slot_hbm, pool_hbm, out_hbm,
    table, length, prompt, pages, owners, queries, slot, gathered, received, picked, traded, staged, pool, others, other_block,
    other_prompt, partial, arrived, numer, stats, out,
    local_sem, prompt_sem, p1_send, p1_recv, z_send, z_recv, t_send, t_recv, r_send, r_recv, c_send, c_recv,
):
    dp = lax.axis_index("dp")
    tp = lax.axis_index("tp")
    core = dp % 2
    z = (dp // 2) % Z
    y_hi = dp // (2 * Z)
    y_lo = tp // X
    x = tp % X
    twin = (dp + 1 - 2 * core, tp)

    def at_y(step):
        y = (y_hi * Y + y_lo + step + 2 * Y) % (2 * Y)
        return (((y // Y) * Z + z) * 2 + core, (y % Y) * X + x)

    def at_x(step):
        return (dp, y_lo * X + (x + step + X) % X)

    def at_z(step):
        return ((y_hi * Z + (z + step + Z) % Z) * 2 + core, tp)

    barrier = pltpu.get_barrier_semaphore()

    def near(i):
        return y_hi * NEAR + (dp + i) % NEAR

    def peer(i, sign):
        dy = (0, 1, 2, -1)[i // X]
        y = (y_hi * Y + y_lo + sign * dy + 2 * Y) % (2 * Y)
        return (((y // Y) * Z + z) * 2 + core, y % Y * X + (x + sign * (i % X) + X) % X)

    partner = ((1 - y_hi) * NEAR + dp % NEAR, tp)

    @each_of(NEAR_ORDER)
    def _(i):
        pl.semaphore_signal(barrier, inc=1, device_id=(near(i), tp), device_id_type=MESH)

    pl.semaphore_signal(barrier, inc=1, device_id=partner, device_id_type=MESH)

    @each_of(TP_ORDER)
    def _(i):
        pl.semaphore_signal(barrier, inc=1, device_id=peer(i, -1), device_id_type=MESH)

    slot_copy, query_in, pool_copy, *small_copies = [
        pltpu.make_async_copy(source, target, local_sem.at[i])
        for i, (source, target) in enumerate((
            (slot_hbm, slot), (queries_hbm, queries), (pool_hbm, pool), (owners_hbm, owners),
            (prompt_hbm, prompt), (pages_hbm, pages), (table_hbm, table), (length_hbm, length),
        ))
    ]
    for copy in [slot_copy, query_in, pool_copy] + small_copies:
        copy.start()

    slot_copy.wait()

    for half in range(2):
        low = slot[0, 32 * half : 32 * half + 16, LAT:WIDTH]
        high = slot[0, 32 * half + 16 : 32 * half + 32, LAT:WIDTH]
        rotary = jnp.concatenate([low, high], axis=1)
        for tile in range(Z):
            lanes, tokens = tile // 2, tile % 2
            first = 32 * half + 16 * tokens
            staged[half, tile, 0] = slot[0, first : first + 16, 128 * lanes : 128 * lanes + 128]
            staged[half, tile, 1] = rotary

    pl.semaphore_wait(barrier, NEAR - 1 + 1 + TP - 1)

    def remote(src, dst, send, recv, device):
        return pltpu.make_async_remote_copy(
            src_ref=src, dst_ref=dst, send_sem=send, recv_sem=recv, device_id=device, device_id_type=MESH
        )

    def spread(i):
        to = near(i)
        return remote(
            staged.at[to % 2, (to // 2) % Z], received.at[dp % NEAR], p1_send.at[i], p1_recv.at[i], (to, tp)
        )

    def spread_in(i):
        source = (dp - i + DP) % NEAR
        return remote(
            staged.at[0, 0], received.at[source], p1_send.at[i], p1_recv.at[i], (near(i), tp)
        )

    @each_of(NEAR_ORDER)
    def _(i):
        spread(i).start()

    received[dp % NEAR] = staged[core, z]
    prompt_copy = remote(prompt_hbm, other_block, c_send.at[0], c_recv.at[0], twin)
    prompt_copy.start()
    query_copy = remote(queries_hbm, others, c_send.at[1], c_recv.at[1], twin)
    query_copy.start()
    for copy in [query_in] + small_copies:
        copy.wait()

    token = lax.broadcasted_iota(jnp.int32, (MAXP * PAGE, HEADS), 0)

    def turned_wide(line):
        return jnp.transpose(jnp.broadcast_to(line, (HEADS, HEADS)))

    def attend(score, values):
        peak = jnp.max(score, axis=0, keepdims=True)
        weight = jnp.exp(score - peak)
        total = jnp.sum(weight, axis=0, keepdims=True)
        numerator = lax.dot_general(
            weight.astype(jnp.bfloat16), values, TN, preferred_element_type=jnp.float32
        )
        return turned_wide(peak), turned_wide(total), numerator

    def private(row):
        keys = jnp.concatenate([pool[table[row, i]] for i in range(MAXP)], axis=0)
        score = lax.dot_general(keys, queries[row], NN, preferred_element_type=jnp.float32)
        score = jnp.where(token < length[row], score * SCALE, BIG_NEGATIVE)
        peak, total, numerator = attend(score, keys[:, :LAT])
        numer[row] = numerator
        stats[row, 0] = peak
        stats[row, 1] = total

    pool_copy.wait()
    private(0)
    prompt_copy.wait_recv()
    to_scalar = pltpu.make_async_copy(other_block, other_prompt, prompt_sem)
    to_scalar.start()

    @each_of(NEAR_ORDER)
    def _(i):
        spread_in(i).wait_recv()

    for p in range(PROMPTS):
        picked[p] = received[owners[p] % NEAR, 0]
    picked[PROMPTS] = received[owners[z] % NEAR, 1]
    trade = remote(picked, traded, c_send.at[4], c_recv.at[4], partner)
    trade.start()
    trade.wait_recv()
    for p in range(POS):
        owner = owners[p] if p < PROMPTS else owners[z]
        gathered[y_lo, x, z, p] = jnp.where(owner // NEAR == y_hi, picked[p], traded[p])

    def z_out(i):
        mine = gathered.at[y_lo, x, z, 0:6]
        return remote(mine, mine, z_send.at[i], z_recv.at[i], at_z(i))

    def z_in(i):
        theirs = gathered.at[y_lo, x, (z - i + Z) % Z, 0:6]
        return remote(theirs, theirs, z_send.at[i], z_recv.at[i], at_z(i))

    def t_out(i):
        mine = gathered.at[y_lo, x, z, 6:9]
        return remote(mine, mine, t_send.at[i], t_recv.at[i], peer(i, 1))

    def t_in(i):
        source = peer(i, -1)[1]
        theirs = gathered.at[source // X, source % X, z, 6:9]
        return remote(theirs, theirs, t_send.at[i], t_recv.at[i], peer(i, 1))

    @each_of(Z_ORDER)
    def _(i):
        z_out(i).start()

    @each_of(TP_ORDER)
    def _(i):
        t_out(i).start()

    private(1)
    started = []

    class Ring:
        def __init__(self, half, place, device, first, size, steps):
            self.half, self.place, self.device = half, place, device
            self.first, self.size, self.steps = first, size, steps

        def copy(self, step, number, way, behind):
            sign = 1 - 2 * way
            origin = (self.place - sign * behind + 2 * self.size) % self.size
            ref = self.half(origin, number if way == 0 else 1 - number)
            index = self.first + 2 * (2 * (step - 1) + number) + way
            return remote(ref, ref, r_send.at[index], r_recv.at[index], self.device(sign))

        def send(self, step, number):
            for way in range(2):
                copy = self.copy(step, number, way, step - 1)
                copy.start()
                started.append(copy)

        def begin(self):
            self.send(1, 0)
            self.send(1, 1)

        def land(self, step, number):
            forward = step + 1 < self.steps or (step + 1 == self.steps and number == 0)
            for way in range(2):
                self.copy(step, number, way, step).wait_recv()
                if forward:
                    copy = self.copy(step + 1, number, way, step)
                    copy.start()
                    started.append(copy)

    ay = Ring(lambda y, h: gathered.at[y, x, 4 * h : 4 * h + 4, 0:3], y_lo, at_y, 0, Y, 2)
    bx = Ring(lambda at, h: gathered.at[y_lo, at, 4 * h : 4 * h + 4, 3:6], x, at_x, 6, X, 2)
    class Slab:
        def __init__(self, piece, place, device, first):
            self.piece, self.place, self.device, self.first = piece, place, device, first

        def copy(self, step, way, behind):
            sign = 1 - 2 * way
            origin = (self.place - sign * behind + 8) % 4
            ref = self.piece(origin, pl.ds(0, Z) if step == 1 else pl.ds(4 * way, 4))
            index = self.first + 2 * (step - 1) + way
            return remote(ref, ref, r_send.at[index], r_recv.at[index], self.device(sign))

        def begin(self):
            for way in range(2):
                copy = self.copy(1, way, 0)
                copy.start()
                started.append(copy)

        def land(self):
            for way in range(2):
                self.copy(1, way, 1).wait_recv()
                copy = self.copy(2, way, 1)
                copy.start()
                started.append(copy)

        def finish(self):
            for way in range(2):
                self.copy(2, way, 2).wait_recv()

    def slab_x(offset):
        row = (y_lo + offset) % Y
        return Slab(lambda at, zs: gathered.at[row, at, zs, 0:3], x, at_x, 26 + 4 * offset)

    def slab_y(offset):
        column = (x + offset) % X
        return Slab(lambda at, zs: gathered.at[at, column, zs, 3:6], y_lo, at_y, 42 + 4 * offset)

    slabs = [(slab_x(offset), slab_y(offset)) for offset in range(4)]

    def each(action, *offsets):
        for offset in offsets:
            for slab in slabs[offset]:
                action(slab)

    cz = Ring(lambda at, h: gathered.at[2 * h : 2 * h + 2, :, at, 6:9], z, at_z, 12, Z, 4)

    @each_of(TP_ORDER)
    def _(i):
        t_in(i).wait_recv()

    cz.begin()
    @each_of(Z_ORDER)
    def _(i):
        z_in(i).wait_recv()

    ay.begin()
    bx.begin()
    each(Slab.begin, 0)

    ay.land(1, 0)
    bx.land(1, 0)
    ay.land(1, 1)
    bx.land(1, 1)
    each(Slab.begin, 3, 1)
    cz.land(1, 0)
    ay.land(2, 0)
    bx.land(2, 0)
    each(Slab.begin, 2)
    cz.land(1, 1)
    each(Slab.land, 0)
    cz.land(2, 0)
    each(Slab.land, 3)
    cz.land(2, 1)
    each(Slab.land, 1)
    cz.land(3, 0)
    each(Slab.land, 2)
    query_copy.wait_recv()
    each(Slab.finish, 0, 3, 1)
    cz.land(3, 1)
    cz.land(4, 0)
    each(Slab.finish, 2)

    page_of = lax.broadcasted_iota(jnp.int32, (512, HEADS), 0) // 16 % TP
    blank = jnp.zeros((ROPE, HEADS), jnp.bfloat16)

    def prefix(query, p):
        latent, rotary = query[:LAT], query[LAT:]
        keys = jnp.concatenate(
            [
                jnp.concatenate(
                    [gathered[:, :, 2 * lanes + tokens, p].reshape(256, 128) for lanes in range(4)], axis=1
                )
                for tokens in range(2)
            ],
            axis=0,
        )
        packed = gathered[:, :, p, PROMPTS].reshape(256, 128)
        turned = [
            lax.dot_general(
                packed, jnp.concatenate(parts, axis=0), NN, preferred_element_type=jnp.float32
            )
            for parts in ([rotary, blank], [blank, rotary])
        ]
        score = lax.dot_general(keys, latent, NN, preferred_element_type=jnp.float32)
        score = (score + jnp.concatenate(turned, axis=0)) * SCALE
        return attend(jnp.where(page_of < pages[p], score, BIG_NEGATIVE), keys)

    to_scalar.wait()
    returns = []
    results = []
    for row in range(ROWS_DEV):
        peak, total, numerator = prefix(others[row], other_prompt[row])
        partial[row, :, :LAT] = numerator
        partial[row, :, LAT : LAT + 128] = peak
        partial[row, :, LAT + 128 :] = total
        back = remote(partial.at[row], arrived.at[row], c_send.at[2 + row], c_recv.at[2 + row], twin)
        back.start()
        returns.append(back)

    for row in range(ROWS_DEV):
        peak, total, numerator = prefix(queries[row], prompt[row])
        returns[row].wait_recv()
        m0, t0 = stats[row, 0], stats[row, 1]
        m1, t1 = arrived[row, :, LAT : LAT + 128], arrived[row, :, LAT + 128 :]
        top = jnp.maximum(jnp.maximum(peak, m0), m1)
        f, f0, f1 = jnp.exp(peak - top), jnp.exp(m0 - top), jnp.exp(m1 - top)
        whole = total * f + t0 * f0 + t1 * f1
        f, f0, f1 = f / whole, f0 / whole, f1 / whole
        for lanes in range(0, LAT, 128):
            part = slice(lanes, lanes + 128)
            summed = numerator[:, part] * f + numer[row, :, part] * f0 + arrived[row, :, part] * f1
            out[row, :, part] = summed.astype(out.dtype)
        result = pltpu.make_async_copy(out.at[row], out_hbm.at[row], local_sem.at[8 + row])
        result.start()
        results.append(result)

    @each_of(NEAR_ORDER)
    def _(i):
        spread(i).wait_send()

    @each_of(Z_ORDER)
    def _(i):
        z_out(i).wait_send()

    @each_of(TP_ORDER)
    def _(i):
        t_out(i).wait_send()

    for copy in started + [trade, prompt_copy, query_copy] + returns:
        copy.wait_send()
    for result in results:
        result.wait()


def on_device(
    q_latent, page_pool, block_table, cache_len, prompt_of_row, prefix_cache, prefix_pages, owners
):
    anywhere = pl.BlockSpec(memory_space=pl.ANY)
    i32 = jnp.int32
    bf16, f32 = jnp.bfloat16, jnp.float32
    dma = pltpu.SemaphoreType.DMA
    return pl.pallas_call(
        kernel,
        out_shape=jax.ShapeDtypeStruct((ROWS_DEV, HEADS, LAT), bf16),
        in_specs=[anywhere] * 8,
        out_specs=anywhere,
        scratch_shapes=[
            pltpu.SMEM((ROWS_DEV, MAXP), i32),
            pltpu.SMEM((ROWS_DEV,), i32),
            pltpu.SMEM((ROWS_DEV,), i32),
            pltpu.SMEM((PROMPTS,), i32),
            pltpu.SMEM((PROMPTS,), i32),
            pltpu.VMEM((ROWS_DEV, WIDTH, HEADS), bf16),
            pltpu.VMEM((1, PAGE, WIDTH), bf16),
            pltpu.VMEM((Y, X, Z, POS, 16, 128), bf16),
            pltpu.VMEM((NEAR, 2, 16, 128), bf16),
            pltpu.VMEM((POS, 16, 128), bf16),
            pltpu.VMEM((POS, 16, 128), bf16),
            pltpu.VMEM((2, Z, 2, 16, 128), bf16),
            pltpu.VMEM((ROWS_DEV * MAXP, PAGE, WIDTH), bf16),
            pltpu.VMEM((ROWS_DEV, WIDTH, HEADS), bf16),
            pltpu.VMEM((ROWS_DEV,), i32),
            pltpu.SMEM((ROWS_DEV,), i32),
            pltpu.VMEM((ROWS_DEV, HEADS, LAT + 256), f32),
            pltpu.VMEM((ROWS_DEV, HEADS, LAT + 256), f32),
            pltpu.VMEM((ROWS_DEV, HEADS, LAT), f32),
            pltpu.VMEM((ROWS_DEV, 2, HEADS, 128), f32),
            pltpu.VMEM((ROWS_DEV, HEADS, LAT), bf16),
            dma((10,)), dma,
            dma((NEAR,)), dma((NEAR,)),
            dma((Z,)), dma((Z,)),
            dma((TP,)), dma((TP,)),
            dma((58,)), dma((58,)),
            dma((5,)), dma((5,)),
        ],
        compiler_params=pltpu.CompilerParams(
            collective_id=0, has_side_effects=True, vmem_limit_bytes=60 * 1024 * 1024
        ),
        cost_estimate=pl.CostEstimate(flops=1200000000, bytes_accessed=3000000, transcendentals=600000),
    )(
        block_table, cache_len, prompt_of_row, prefix_pages, owners,
        jnp.swapaxes(q_latent, 1, 2), prefix_cache, page_pool,
    )


def solution(mesh):
    placed = (
        P(("dp", "tp"), None, None),
        P(("dp", "tp"), None, None),
        P(("dp", "tp"), None),
        P(("dp", "tp")),
        P(("dp", "tp")),
        P("dp", "tp", None),
        P(),
        P(),
    )
    return jax.shard_map(
        on_device,
        mesh=mesh,
        in_specs=placed,
        out_specs=P(("dp", "tp"), None, None),
        check_vma=False,
    )
```

```python
import jax
import jax.numpy as jnp
from jax import lax
from jax.experimental import pallas as pl
from jax.experimental.pallas import tpu as pltpu
from jax.sharding import PartitionSpec as P

LAT = 512
ROPE = 64
WIDTH = LAT + ROPE
HEADS = 128
PAGE = 64
MAXP = 16
PROMPTS = 8
ROWS_DEV = 2
X, Y, Z, DP, TP = 4, 4, 8, 32, 16
NEAR = 2 * Z
NEAR_ORDER = sorted(range(1, NEAR), key=lambda i: -min(i, NEAR - i))
Z_ORDER = (3, 5, 2, 6, 1, 7)
TP_ORDER = [4 * dy + dx for dx in (2, 1, 3, 0) for dy in (2, 1, 3, 0)][:-1]
POS = PROMPTS + 1
SCALE = 192.0 ** (-0.5)
BIG_NEGATIVE = -1e30
MESH = pl.DeviceIdType.MESH
TN = (((0,), (0,)), ((), ()))
NN = (((1,), (0,)), ((), ()))


def each_of(numbers):
    def run(body):
        for i in numbers:
            body(i)

    return run


def kernel(
    table_hbm, length_hbm, prompt_hbm, pages_hbm, owners_hbm, queries_hbm, slot_hbm, pool_hbm, out_hbm,
    table, length, prompt, pages, owners, queries, slot, gathered, received, picked, traded, staged, pool, others, other_block,
    other_prompt, partial, arrived, numer, stats, out,
    local_sem, prompt_sem, p1_send, p1_recv, z_send, z_recv, t_send, t_recv, r_send, r_recv, c_send, c_recv,
):
    dp = lax.axis_index("dp")
    tp = lax.axis_index("tp")
    core = dp % 2
    z = (dp // 2) % Z
    y_hi = dp // (2 * Z)
    y_lo = tp // X
    x = tp % X
    twin = (dp + 1 - 2 * core, tp)

    def at_y(step):
        y = (y_hi * Y + y_lo + step + 2 * Y) % (2 * Y)
        return (((y // Y) * Z + z) * 2 + core, (y % Y) * X + x)

    def at_x(step):
        return (dp, y_lo * X + (x + step + X) % X)

    def at_z(step):
        return ((y_hi * Z + (z + step + Z) % Z) * 2 + core, tp)

    barrier = pltpu.get_barrier_semaphore()

    def near(i):
        return y_hi * NEAR + (dp + i) % NEAR

    def peer(i, sign):
        dy = (0, 1, 2, -1)[i // X]
        y = (y_hi * Y + y_lo + sign * dy + 2 * Y) % (2 * Y)
        return (((y // Y) * Z + z) * 2 + core, y % Y * X + (x + sign * (i % X) + X) % X)

    partner = ((1 - y_hi) * NEAR + dp % NEAR, tp)

    @each_of(NEAR_ORDER)
    def _(i):
        pl.semaphore_signal(barrier, inc=1, device_id=(near(i), tp), device_id_type=MESH)

    pl.semaphore_signal(barrier, inc=1, device_id=partner, device_id_type=MESH)

    @each_of(TP_ORDER)
    def _(i):
        pl.semaphore_signal(barrier, inc=1, device_id=peer(i, -1), device_id_type=MESH)

    slot_copy, query_in, pool_copy, *small_copies = [
        pltpu.make_async_copy(source, target, local_sem.at[i])
        for i, (source, target) in enumerate((
            (slot_hbm, slot), (queries_hbm, queries), (pool_hbm, pool), (owners_hbm, owners),
            (prompt_hbm, prompt), (pages_hbm, pages), (table_hbm, table), (length_hbm, length),
        ))
    ]
    for copy in [slot_copy, query_in, pool_copy] + small_copies:
        copy.start()

    slot_copy.wait()

    for half in range(2):
        low = slot[0, 32 * half : 32 * half + 16, LAT:WIDTH]
        high = slot[0, 32 * half + 16 : 32 * half + 32, LAT:WIDTH]
        rotary = jnp.concatenate([low, high], axis=1)
        for tile in range(Z):
            lanes, tokens = tile // 2, tile % 2
            first = 32 * half + 16 * tokens
            staged[half, tile, 0] = slot[0, first : first + 16, 128 * lanes : 128 * lanes + 128]
            staged[half, tile, 1] = rotary

    pl.semaphore_wait(barrier, NEAR - 1 + 1 + TP - 1)

    def remote(src, dst, send, recv, device):
        return pltpu.make_async_remote_copy(
            src_ref=src, dst_ref=dst, send_sem=send, recv_sem=recv, device_id=device, device_id_type=MESH
        )

    def spread(i):
        to = near(i)
        return remote(
            staged.at[to % 2, (to // 2) % Z], received.at[dp % NEAR], p1_send.at[i], p1_recv.at[i], (to, tp)
        )

    def spread_in(i):
        source = (dp - i + DP) % NEAR
        return remote(
            staged.at[0, 0], received.at[source], p1_send.at[i], p1_recv.at[i], (near(i), tp)
        )

    @each_of(NEAR_ORDER)
    def _(i):
        spread(i).start()

    received[dp % NEAR] = staged[core, z]
    prompt_copy = remote(prompt_hbm, other_block, c_send.at[0], c_recv.at[0], twin)
    prompt_copy.start()
    query_copy = remote(queries_hbm, others, c_send.at[1], c_recv.at[1], twin)
    query_copy.start()
    for copy in [query_in] + small_copies:
        copy.wait()

    token = lax.broadcasted_iota(jnp.int32, (MAXP * PAGE, HEADS), 0)

    def turned_wide(line):
        return jnp.transpose(jnp.broadcast_to(line, (HEADS, HEADS)))

    def attend(score, values):
        peak = jnp.max(score, axis=0, keepdims=True)
        weight = jnp.exp(score - peak)
        total = jnp.sum(weight, axis=0, keepdims=True)
        numerator = lax.dot_general(
            weight.astype(jnp.bfloat16), values, TN, preferred_element_type=jnp.float32
        )
        return turned_wide(peak), turned_wide(total), numerator

    def private(row):
        keys = jnp.concatenate([pool[table[row, i]] for i in range(MAXP)], axis=0)
        score = lax.dot_general(keys, queries[row], NN, preferred_element_type=jnp.float32)
        score = jnp.where(token < length[row], score * SCALE, BIG_NEGATIVE)
        peak, total, numerator = attend(score, keys[:, :LAT])
        numer[row] = numerator
        stats[row, 0] = peak
        stats[row, 1] = total

    pool_copy.wait()
    private(0)
    prompt_copy.wait_recv()
    to_scalar = pltpu.make_async_copy(other_block, other_prompt, prompt_sem)
    to_scalar.start()

    @each_of(NEAR_ORDER)
    def _(i):
        spread_in(i).wait_recv()

    for p in range(PROMPTS):
        picked[p] = received[owners[p] % NEAR, 0]
    picked[PROMPTS] = received[owners[z] % NEAR, 1]
    trade = remote(picked, traded, c_send.at[4], c_recv.at[4], partner)
    trade.start()
    trade.wait_recv()
    for p in range(POS):
        owner = owners[p] if p < PROMPTS else owners[z]
        gathered[y_lo, x, z, p] = jnp.where(owner // NEAR == y_hi, picked[p], traded[p])

    def z_out(i):
        mine = gathered.at[y_lo, x, z, 0:6]
        return remote(mine, mine, z_send.at[i], z_recv.at[i], at_z(i))

    def z_in(i):
        theirs = gathered.at[y_lo, x, (z - i + Z) % Z, 0:6]
        return remote(theirs, theirs, z_send.at[i], z_recv.at[i], at_z(i))

    def z_pass(sign, arriving):
        origin = (z - (4 if arriving else 3) * sign + Z) % Z
        low, index = (0, 4) if sign == 1 else (3, 0)
        ref = gathered.at[y_lo, x, origin, low : low + 3]
        return remote(ref, ref, z_send.at[index], z_recv.at[index], at_z(sign))

    def t_out(i):
        mine = gathered.at[y_lo, x, z, 6:9]
        return remote(mine, mine, t_send.at[i], t_recv.at[i], peer(i, 1))

    def t_in(i):
        source = peer(i, -1)[1]
        theirs = gathered.at[source // X, source % X, z, 6:9]
        return remote(theirs, theirs, t_send.at[i], t_recv.at[i], peer(i, 1))

    @each_of(Z_ORDER)
    def _(i):
        z_out(i).start()

    @each_of(TP_ORDER)
    def _(i):
        t_out(i).start()

    private(1)
    started = []

    class Ring:
        def __init__(self, half, place, device, first, size, steps):
            self.half, self.place, self.device = half, place, device
            self.first, self.size, self.steps = first, size, steps

        def copy(self, step, number, way, behind):
            sign = 1 - 2 * way
            origin = (self.place - sign * behind + 2 * self.size) % self.size
            ref = self.half(origin, number if way == 0 else 1 - number)
            index = self.first + 2 * (2 * (step - 1) + number) + way
            return remote(ref, ref, r_send.at[index], r_recv.at[index], self.device(sign))

        def send(self, step, number):
            for way in range(2):
                copy = self.copy(step, number, way, step - 1)
                copy.start()
                started.append(copy)

        def begin(self):
            self.send(1, 0)
            self.send(1, 1)

        def land(self, step, number):
            forward = step + 1 < self.steps or (step + 1 == self.steps and number == 0)
            for way in range(2):
                self.copy(step, number, way, step).wait_recv()
                if forward:
                    copy = self.copy(step + 1, number, way, step)
                    copy.start()
                    started.append(copy)

    ay = Ring(lambda y, h: gathered.at[y, x, 4 * h : 4 * h + 4, 0:3], y_lo, at_y, 0, Y, 2)
    bx = Ring(lambda at, h: gathered.at[y_lo, at, 4 * h : 4 * h + 4, 3:6], x, at_x, 6, X, 2)
    class Slab:
        def __init__(self, piece, place, device, first):
            self.piece, self.place, self.device, self.first = piece, place, device, first

        def copy(self, step, way, behind):
            sign = 1 - 2 * way
            origin = (self.place - sign * behind + 8) % 4
            ref = self.piece(origin, pl.ds(0, Z) if step == 1 else pl.ds(4 * way, 4))
            index = self.first + 2 * (step - 1) + way
            return remote(ref, ref, r_send.at[index], r_recv.at[index], self.device(sign))

        def begin(self):
            for way in range(2):
                copy = self.copy(1, way, 0)
                copy.start()
                started.append(copy)

        def land(self):
            for way in range(2):
                self.copy(1, way, 1).wait_recv()
                copy = self.copy(2, way, 1)
                copy.start()
                started.append(copy)

        def finish(self):
            for way in range(2):
                self.copy(2, way, 2).wait_recv()

    def slab_x(offset):
        row = (y_lo + offset) % Y
        return Slab(lambda at, zs: gathered.at[row, at, zs, 0:3], x, at_x, 26 + 4 * offset)

    def slab_y(offset):
        column = (x + offset) % X
        return Slab(lambda at, zs: gathered.at[at, column, zs, 3:6], y_lo, at_y, 42 + 4 * offset)

    slabs = [(slab_x(offset), slab_y(offset)) for offset in range(4)]

    def each(action, *offsets):
        for offset in offsets:
            for slab in slabs[offset]:
                action(slab)

    cz = Ring(lambda at, h: gathered.at[2 * h : 2 * h + 2, :, at, 6:9], z, at_z, 12, Z, 4)

    @each_of(Z_ORDER)
    def _(i):
        z_in(i).wait_recv()
        if i in (3, 5):
            z_pass(4 - i, False).start()

    for sign in (1, -1):
        z_pass(sign, True).wait_recv()

    ay.begin()
    bx.begin()
    each(Slab.begin, 0)

    @each_of(TP_ORDER)
    def _(i):
        t_in(i).wait_recv()

    cz.begin()
    ay.land(1, 0)
    bx.land(1, 0)
    ay.land(1, 1)
    bx.land(1, 1)
    each(Slab.begin, 3, 1)
    ay.land(2, 0)
    bx.land(2, 0)
    each(Slab.begin, 2)
    cz.land(1, 0)
    cz.land(1, 1)
    each(Slab.land, 0)
    cz.land(2, 0)
    each(Slab.land, 3)
    cz.land(2, 1)
    each(Slab.land, 1)
    cz.land(3, 0)
    each(Slab.land, 2)
    query_copy.wait_recv()
    each(Slab.finish, 0, 3, 1)
    cz.land(3, 1)
    cz.land(4, 0)
    each(Slab.finish, 2)

    page_of = lax.broadcasted_iota(jnp.int32, (512, HEADS), 0) // 16 % TP
    blank = jnp.zeros((ROPE, HEADS), jnp.bfloat16)

    def prefix(query, p):
        latent, rotary = query[:LAT], query[LAT:]
        keys = jnp.concatenate(
            [
                jnp.concatenate(
                    [gathered[:, :, 2 * lanes + tokens, p].reshape(256, 128) for lanes in range(4)], axis=1
                )
                for tokens in range(2)
            ],
            axis=0,
        )
        packed = gathered[:, :, p, PROMPTS].reshape(256, 128)
        turned = [
            lax.dot_general(
                packed, jnp.concatenate(parts, axis=0), NN, preferred_element_type=jnp.float32
            )
            for parts in ([rotary, blank], [blank, rotary])
        ]
        score = lax.dot_general(keys, latent, NN, preferred_element_type=jnp.float32)
        score = (score + jnp.concatenate(turned, axis=0)) * SCALE
        return attend(jnp.where(page_of < pages[p], score, BIG_NEGATIVE), keys)

    to_scalar.wait()
    returns = []
    results = []
    for row in range(ROWS_DEV):
        peak, total, numerator = prefix(others[row], other_prompt[row])
        partial[row, :, :LAT] = numerator
        partial[row, :, LAT : LAT + 128] = peak
        partial[row, :, LAT + 128 :] = total
        back = remote(partial.at[row], arrived.at[row], c_send.at[2 + row], c_recv.at[2 + row], twin)
        back.start()
        returns.append(back)

    for row in range(ROWS_DEV):
        peak, total, numerator = prefix(queries[row], prompt[row])
        returns[row].wait_recv()
        m0, t0 = stats[row, 0], stats[row, 1]
        m1, t1 = arrived[row, :, LAT : LAT + 128], arrived[row, :, LAT + 128 :]
        top = jnp.maximum(jnp.maximum(peak, m0), m1)
        f, f0, f1 = jnp.exp(peak - top), jnp.exp(m0 - top), jnp.exp(m1 - top)
        whole = total * f + t0 * f0 + t1 * f1
        f, f0, f1 = f / whole, f0 / whole, f1 / whole
        for lanes in range(0, LAT, 128):
            part = slice(lanes, lanes + 128)
            summed = numerator[:, part] * f + numer[row, :, part] * f0 + arrived[row, :, part] * f1
            out[row, :, part] = summed.astype(out.dtype)
        result = pltpu.make_async_copy(out.at[row], out_hbm.at[row], local_sem.at[8 + row])
        result.start()
        results.append(result)

    @each_of(NEAR_ORDER)
    def _(i):
        spread(i).wait_send()

    @each_of(Z_ORDER)
    def _(i):
        z_out(i).wait_send()

    for sign in (1, -1):
        z_pass(sign, False).wait_send()

    @each_of(TP_ORDER)
    def _(i):
        t_out(i).wait_send()

    for copy in started + [trade, prompt_copy, query_copy] + returns:
        copy.wait_send()
    for result in results:
        result.wait()


def on_device(
    q_latent, page_pool, block_table, cache_len, prompt_of_row, prefix_cache, prefix_pages, owners
):
    anywhere = pl.BlockSpec(memory_space=pl.ANY)
    i32 = jnp.int32
    bf16, f32 = jnp.bfloat16, jnp.float32
    dma = pltpu.SemaphoreType.DMA
    return pl.pallas_call(
        kernel,
        out_shape=jax.ShapeDtypeStruct((ROWS_DEV, HEADS, LAT), bf16),
        in_specs=[anywhere] * 8,
        out_specs=anywhere,
        scratch_shapes=[
            pltpu.SMEM((ROWS_DEV, MAXP), i32),
            pltpu.SMEM((ROWS_DEV,), i32),
            pltpu.SMEM((ROWS_DEV,), i32),
            pltpu.SMEM((PROMPTS,), i32),
            pltpu.SMEM((PROMPTS,), i32),
            pltpu.VMEM((ROWS_DEV, WIDTH, HEADS), bf16),
            pltpu.VMEM((1, PAGE, WIDTH), bf16),
            pltpu.VMEM((Y, X, Z, POS, 16, 128), bf16),
            pltpu.VMEM((NEAR, 2, 16, 128), bf16),
            pltpu.VMEM((POS, 16, 128), bf16),
            pltpu.VMEM((POS, 16, 128), bf16),
            pltpu.VMEM((2, Z, 2, 16, 128), bf16),
            pltpu.VMEM((ROWS_DEV * MAXP, PAGE, WIDTH), bf16),
            pltpu.VMEM((ROWS_DEV, WIDTH, HEADS), bf16),
            pltpu.VMEM((ROWS_DEV,), i32),
            pltpu.SMEM((ROWS_DEV,), i32),
            pltpu.VMEM((ROWS_DEV, HEADS, LAT + 256), f32),
            pltpu.VMEM((ROWS_DEV, HEADS, LAT + 256), f32),
            pltpu.VMEM((ROWS_DEV, HEADS, LAT), f32),
            pltpu.VMEM((ROWS_DEV, 2, HEADS, 128), f32),
            pltpu.VMEM((ROWS_DEV, HEADS, LAT), bf16),
            dma((10,)), dma,
            dma((NEAR,)), dma((NEAR,)),
            dma((Z,)), dma((Z,)),
            dma((TP,)), dma((TP,)),
            dma((58,)), dma((58,)),
            dma((5,)), dma((5,)),
        ],
        compiler_params=pltpu.CompilerParams(
            collective_id=0, has_side_effects=True, vmem_limit_bytes=60 * 1024 * 1024
        ),
        cost_estimate=pl.CostEstimate(flops=1200000000, bytes_accessed=3000000, transcendentals=600000),
    )(
        block_table, cache_len, prompt_of_row, prefix_pages, owners,
        jnp.swapaxes(q_latent, 1, 2), prefix_cache, page_pool,
    )


def solution(mesh):
    placed = (
        P(("dp", "tp"), None, None),
        P(("dp", "tp"), None, None),
        P(("dp", "tp"), None),
        P(("dp", "tp")),
        P(("dp", "tp")),
        P("dp", "tp", None),
        P(),
        P(),
    )
    return jax.shard_map(
        on_device,
        mesh=mesh,
        in_specs=placed,
        out_specs=P(("dp", "tp"), None, None),
        check_vma=False,
    )
```

```python
import jax
import jax.numpy as jnp
from jax import lax
from jax.experimental import pallas as pl
from jax.experimental.pallas import tpu as pltpu
from jax.sharding import PartitionSpec as P

LAT = 512
ROPE = 64
WIDTH = LAT + ROPE
HEADS = 128
PAGE = 64
MAXP = 16
PROMPTS = 8
ROWS_DEV = 2
X, Y, Z, DP, TP = 4, 4, 8, 32, 16
NEAR = 2 * Z
NEAR_ORDER = sorted(range(1, NEAR), key=lambda i: -min(i, NEAR - i))
Z_ORDER = sorted(range(1, Z), key=lambda i: -min(i, Z - i))
TP_ORDER = [4 * dy + dx for dx in (2, 1, 3, 0) for dy in (2, 1, 3, 0)][:-1]
POS = PROMPTS + 1
SCALE = 192.0 ** (-0.5)
BIG_NEGATIVE = -1e30
MESH = pl.DeviceIdType.MESH
TN = (((0,), (0,)), ((), ()))
NN = (((1,), (0,)), ((), ()))


def each_of(numbers):
    def run(body):
        for i in numbers:
            body(i)

    return run


def kernel(
    table_hbm, length_hbm, prompt_hbm, pages_hbm, owners_hbm, queries_hbm, slot_hbm, pool_hbm, out_hbm,
    table, length, prompt, pages, owners, queries, slot, gathered, received, picked, traded, staged, pool, others, other_block,
    other_prompt, partial, arrived, numer, stats, out,
    local_sem, prompt_sem, p1_send, p1_recv, z_send, z_recv, t_send, t_recv, r_send, r_recv, c_send, c_recv,
):
    dp = lax.axis_index("dp")
    tp = lax.axis_index("tp")
    core = dp % 2
    z = (dp // 2) % Z
    y_hi = dp // (2 * Z)
    y_lo = tp // X
    x = tp % X
    twin = (dp + 1 - 2 * core, tp)

    def at_y(step):
        y = (y_hi * Y + y_lo + step + 2 * Y) % (2 * Y)
        return (((y // Y) * Z + z) * 2 + core, (y % Y) * X + x)

    def at_x(step):
        return (dp, y_lo * X + (x + step + X) % X)

    def at_z(step):
        return ((y_hi * Z + (z + step + Z) % Z) * 2 + core, tp)

    barrier = pltpu.get_barrier_semaphore()

    def near(i):
        return y_hi * NEAR + (dp + i) % NEAR

    def peer(i, sign):
        dy = (0, 1, 2, -1)[i // X]
        y = (y_hi * Y + y_lo + sign * dy + 2 * Y) % (2 * Y)
        return (((y // Y) * Z + z) * 2 + core, y % Y * X + (x + sign * (i % X) + X) % X)

    partner = ((1 - y_hi) * NEAR + dp % NEAR, tp)

    @each_of(NEAR_ORDER)
    def _(i):
        pl.semaphore_signal(barrier, inc=1, device_id=(near(i), tp), device_id_type=MESH)

    pl.semaphore_signal(barrier, inc=1, device_id=partner, device_id_type=MESH)

    @each_of(TP_ORDER)
    def _(i):
        pl.semaphore_signal(barrier, inc=1, device_id=peer(i, -1), device_id_type=MESH)

    slot_copy, query_in, pool_copy, *small_copies = [
        pltpu.make_async_copy(source, target, local_sem.at[i])
        for i, (source, target) in enumerate((
            (slot_hbm, slot), (queries_hbm, queries), (pool_hbm, pool), (owners_hbm, owners),
            (prompt_hbm, prompt), (pages_hbm, pages), (table_hbm, table), (length_hbm, length),
        ))
    ]
    for copy in [slot_copy, query_in, pool_copy] + small_copies:
        copy.start()

    slot_copy.wait()

    for half in range(2):
        low = slot[0, 32 * half : 32 * half + 16, LAT:WIDTH]
        high = slot[0, 32 * half + 16 : 32 * half + 32, LAT:WIDTH]
        rotary = jnp.concatenate([low, high], axis=1)
        for tile in range(Z):
            lanes, tokens = tile // 2, tile % 2
            first = 32 * half + 16 * tokens
            staged[half, tile, 0] = slot[0, first : first + 16, 128 * lanes : 128 * lanes + 128]
            staged[half, tile, 1] = rotary

    pl.semaphore_wait(barrier, NEAR - 1 + 1 + TP - 1)

    def remote(src, dst, send, recv, device):
        return pltpu.make_async_remote_copy(
            src_ref=src, dst_ref=dst, send_sem=send, recv_sem=recv, device_id=device, device_id_type=MESH
        )

    def spread(i):
        to = near(i)
        return remote(
            staged.at[to % 2, (to // 2) % Z], received.at[dp % NEAR], p1_send.at[i], p1_recv.at[i], (to, tp)
        )

    def spread_in(i):
        source = (dp - i + DP) % NEAR
        return remote(
            staged.at[0, 0], received.at[source], p1_send.at[i], p1_recv.at[i], (near(i), tp)
        )

    @each_of(NEAR_ORDER)
    def _(i):
        spread(i).start()

    received[dp % NEAR] = staged[core, z]
    prompt_copy = remote(prompt_hbm, other_block, c_send.at[0], c_recv.at[0], twin)
    prompt_copy.start()
    query_copy = remote(queries_hbm, others, c_send.at[1], c_recv.at[1], twin)
    query_copy.start()
    for copy in [query_in] + small_copies:
        copy.wait()

    token = lax.broadcasted_iota(jnp.int32, (MAXP * PAGE, HEADS), 0)

    def turned_wide(line):
        return jnp.transpose(jnp.broadcast_to(line, (HEADS, HEADS)))

    def attend(score, values):
        peak = jnp.max(score, axis=0, keepdims=True)
        weight = jnp.exp(score - peak)
        total = jnp.sum(weight, axis=0, keepdims=True)
        numerator = lax.dot_general(
            weight.astype(jnp.bfloat16), values, TN, preferred_element_type=jnp.float32
        )
        return turned_wide(peak), turned_wide(total), numerator

    def private(row):
        keys = jnp.concatenate([pool[table[row, i]] for i in range(MAXP)], axis=0)
        score = lax.dot_general(keys, queries[row], NN, preferred_element_type=jnp.float32)
        score = jnp.where(token < length[row], score * SCALE, BIG_NEGATIVE)
        peak, total, numerator = attend(score, keys[:, :LAT])
        numer[row] = numerator
        stats[row, 0] = peak
        stats[row, 1] = total

    pool_copy.wait()
    private(0)
    prompt_copy.wait_recv()
    to_scalar = pltpu.make_async_copy(other_block, other_prompt, prompt_sem)
    to_scalar.start()

    @each_of(NEAR_ORDER)
    def _(i):
        spread_in(i).wait_recv()

    for p in range(PROMPTS):
        picked[p] = received[owners[p] % NEAR, 0]
    picked[PROMPTS] = received[owners[z] % NEAR, 1]
    trade = remote(picked, traded, c_send.at[4], c_recv.at[4], partner)
    trade.start()
    trade.wait_recv()
    for p in range(POS):
        owner = owners[p] if p < PROMPTS else owners[z]
        gathered[y_lo, x, z, p] = jnp.where(owner // NEAR == y_hi, picked[p], traded[p])

    def z_out(i):
        mine = gathered.at[y_lo, x, z, 0:6]
        return remote(mine, mine, z_send.at[i], z_recv.at[i], at_z(i))

    def z_in(i):
        theirs = gathered.at[y_lo, x, (z - i + Z) % Z, 0:6]
        return remote(theirs, theirs, z_send.at[i], z_recv.at[i], at_z(i))

    def t_out(i):
        mine = gathered.at[y_lo, x, z, 6:9]
        return remote(mine, mine, t_send.at[i], t_recv.at[i], peer(i, 1))

    def t_in(i):
        source = peer(i, -1)[1]
        theirs = gathered.at[source // X, source % X, z, 6:9]
        return remote(theirs, theirs, t_send.at[i], t_recv.at[i], peer(i, 1))

    @each_of(Z_ORDER)
    def _(i):
        z_out(i).start()

    @each_of(TP_ORDER)
    def _(i):
        t_out(i).start()

    private(1)
    started = []

    class Ring:
        def __init__(self, half, place, device, first, size, steps):
            self.half, self.place, self.device = half, place, device
            self.first, self.size, self.steps = first, size, steps

        def copy(self, step, number, way, behind):
            sign = 1 - 2 * way
            origin = (self.place - sign * behind + 2 * self.size) % self.size
            ref = self.half(origin, number if way == 0 else 1 - number)
            index = self.first + 2 * (2 * (step - 1) + number) + way
            return remote(ref, ref, r_send.at[index], r_recv.at[index], self.device(sign))

        def send(self, step, number):
            for way in range(2):
                copy = self.copy(step, number, way, step - 1)
                copy.start()
                started.append(copy)

        def begin(self):
            self.send(1, 0)
            self.send(1, 1)

        def land(self, step, number):
            forward = step + 1 < self.steps or (step + 1 == self.steps and number == 0)
            for way in range(2):
                self.copy(step, number, way, step).wait_recv()
                if forward:
                    copy = self.copy(step + 1, number, way, step)
                    copy.start()
                    started.append(copy)

    ay = Ring(lambda y, h: gathered.at[y, x, 4 * h : 4 * h + 4, 0:3], y_lo, at_y, 0, Y, 2)
    bx = Ring(lambda at, h: gathered.at[y_lo, at, 4 * h : 4 * h + 4, 3:6], x, at_x, 6, X, 2)
    class Slab:
        def __init__(self, piece, place, device, first):
            self.piece, self.place, self.device, self.first = piece, place, device, first

        def copy(self, step, way, behind):
            sign = 1 - 2 * way
            origin = (self.place - sign * behind + 8) % 4
            ref = self.piece(origin, pl.ds(0, Z) if step == 1 else pl.ds(4 * way, 4))
            index = self.first + 2 * (step - 1) + way
            return remote(ref, ref, r_send.at[index], r_recv.at[index], self.device(sign))

        def begin(self):
            for way in range(2):
                copy = self.copy(1, way, 0)
                copy.start()
                started.append(copy)

        def land(self):
            for way in range(2):
                self.copy(1, way, 1).wait_recv()
                copy = self.copy(2, way, 1)
                copy.start()
                started.append(copy)

        def finish(self):
            for way in range(2):
                self.copy(2, way, 2).wait_recv()

    def slab_x(offset):
        row = (y_lo + offset) % Y
        return Slab(lambda at, zs: gathered.at[row, at, zs, 0:3], x, at_x, 26 + 4 * offset)

    def slab_y(offset):
        column = (x + offset) % X
        return Slab(lambda at, zs: gathered.at[at, column, zs, 3:6], y_lo, at_y, 42 + 4 * offset)

    slabs = [(slab_x(offset), slab_y(offset)) for offset in range(4)]

    def each(action, *offsets):
        for offset in offsets:
            for slab in slabs[offset]:
                action(slab)

    cz = Ring(lambda at, h: gathered.at[2 * h : 2 * h + 2, :, at, 6:9], z, at_z, 12, Z, 4)

    @each_of(TP_ORDER)
    def _(i):
        t_in(i).wait_recv()

    cz.begin()
    @each_of(Z_ORDER)
    def _(i):
        z_in(i).wait_recv()

    ay.begin()
    bx.begin()
    each(Slab.begin, 0)

    cz.land(1, 0)
    ay.land(1, 0)
    bx.land(1, 0)
    ay.land(1, 1)
    bx.land(1, 1)
    each(Slab.begin, 3, 1)
    cz.land(1, 1)
    each(Slab.land, 0)
    ay.land(2, 0)
    bx.land(2, 0)
    each(Slab.begin, 2)
    cz.land(2, 0)
    each(Slab.land, 3)
    cz.land(2, 1)
    each(Slab.land, 1)
    cz.land(3, 0)
    each(Slab.land, 2)
    query_copy.wait_recv()
    each(Slab.finish, 0, 3, 1)
    cz.land(3, 1)
    cz.land(4, 0)
    each(Slab.finish, 2)

    page_of = lax.broadcasted_iota(jnp.int32, (512, HEADS), 0) // 16 % TP
    blank = jnp.zeros((ROPE, HEADS), jnp.bfloat16)

    def prefix(query, p):
        latent, rotary = query[:LAT], query[LAT:]
        keys = jnp.concatenate(
            [
                jnp.concatenate(
                    [gathered[:, :, 2 * lanes + tokens, p].reshape(256, 128) for lanes in range(4)], axis=1
                )
                for tokens in range(2)
            ],
            axis=0,
        )
        packed = gathered[:, :, p, PROMPTS].reshape(256, 128)
        turned = [
            lax.dot_general(
                packed, jnp.concatenate(parts, axis=0), NN, preferred_element_type=jnp.float32
            )
            for parts in ([rotary, blank], [blank, rotary])
        ]
        score = lax.dot_general(keys, latent, NN, preferred_element_type=jnp.float32)
        score = (score + jnp.concatenate(turned, axis=0)) * SCALE
        return attend(jnp.where(page_of < pages[p], score, BIG_NEGATIVE), keys)

    to_scalar.wait()
    returns = []
    results = []
    for row in range(ROWS_DEV):
        peak, total, numerator = prefix(others[row], other_prompt[row])
        partial[row, :, :LAT] = numerator
        partial[row, :, LAT : LAT + 128] = peak
        partial[row, :, LAT + 128 :] = total
        back = remote(partial.at[row], arrived.at[row], c_send.at[2 + row], c_recv.at[2 + row], twin)
        back.start()
        returns.append(back)

    for row in range(ROWS_DEV):
        peak, total, numerator = prefix(queries[row], prompt[row])
        returns[row].wait_recv()
        m0, t0 = stats[row, 0], stats[row, 1]
        m1, t1 = arrived[row, :, LAT : LAT + 128], arrived[row, :, LAT + 128 :]
        top = jnp.maximum(jnp.maximum(peak, m0), m1)
        f, f0, f1 = jnp.exp(peak - top), jnp.exp(m0 - top), jnp.exp(m1 - top)
        whole = total * f + t0 * f0 + t1 * f1
        f, f0, f1 = f / whole, f0 / whole, f1 / whole
        for lanes in range(0, LAT, 128):
            part = slice(lanes, lanes + 128)
            summed = numerator[:, part] * f + numer[row, :, part] * f0 + arrived[row, :, part] * f1
            out[row, :, part] = summed.astype(out.dtype)
        result = pltpu.make_async_copy(out.at[row], out_hbm.at[row], local_sem.at[8 + row])
        result.start()
        results.append(result)

    @each_of(NEAR_ORDER)
    def _(i):
        spread(i).wait_send()

    @each_of(Z_ORDER)
    def _(i):
        z_out(i).wait_send()

    @each_of(TP_ORDER)
    def _(i):
        t_out(i).wait_send()

    for copy in started + [trade, prompt_copy, query_copy] + returns:
        copy.wait_send()
    for result in results:
        result.wait()


def on_device(
    q_latent, page_pool, block_table, cache_len, prompt_of_row, prefix_cache, prefix_pages, owners
):
    anywhere = pl.BlockSpec(memory_space=pl.ANY)
    i32 = jnp.int32
    bf16, f32 = jnp.bfloat16, jnp.float32
    dma = pltpu.SemaphoreType.DMA
    return pl.pallas_call(
        kernel,
        out_shape=jax.ShapeDtypeStruct((ROWS_DEV, HEADS, LAT), bf16),
        in_specs=[anywhere] * 8,
        out_specs=anywhere,
        scratch_shapes=[
            pltpu.SMEM((ROWS_DEV, MAXP), i32),
            pltpu.SMEM((ROWS_DEV,), i32),
            pltpu.SMEM((ROWS_DEV,), i32),
            pltpu.SMEM((PROMPTS,), i32),
            pltpu.SMEM((PROMPTS,), i32),
            pltpu.VMEM((ROWS_DEV, WIDTH, HEADS), bf16),
            pltpu.VMEM((1, PAGE, WIDTH), bf16),
            pltpu.VMEM((Y, X, Z, POS, 16, 128), bf16),
            pltpu.VMEM((NEAR, 2, 16, 128), bf16),
            pltpu.VMEM((POS, 16, 128), bf16),
            pltpu.VMEM((POS, 16, 128), bf16),
            pltpu.VMEM((2, Z, 2, 16, 128), bf16),
            pltpu.VMEM((ROWS_DEV * MAXP, PAGE, WIDTH), bf16),
            pltpu.VMEM((ROWS_DEV, WIDTH, HEADS), bf16),
            pltpu.VMEM((ROWS_DEV,), i32),
            pltpu.SMEM((ROWS_DEV,), i32),
            pltpu.VMEM((ROWS_DEV, HEADS, LAT + 256), f32),
            pltpu.VMEM((ROWS_DEV, HEADS, LAT + 256), f32),
            pltpu.VMEM((ROWS_DEV, HEADS, LAT), f32),
            pltpu.VMEM((ROWS_DEV, 2, HEADS, 128), f32),
            pltpu.VMEM((ROWS_DEV, HEADS, LAT), bf16),
            dma((10,)), dma,
            dma((NEAR,)), dma((NEAR,)),
            dma((Z,)), dma((Z,)),
            dma((TP,)), dma((TP,)),
            dma((58,)), dma((58,)),
            dma((5,)), dma((5,)),
        ],
        compiler_params=pltpu.CompilerParams(
            collective_id=0, has_side_effects=True, vmem_limit_bytes=60 * 1024 * 1024
        ),
        cost_estimate=pl.CostEstimate(flops=1200000000, bytes_accessed=3000000, transcendentals=600000),
    )(
        block_table, cache_len, prompt_of_row, prefix_pages, owners,
        jnp.swapaxes(q_latent, 1, 2), prefix_cache, page_pool,
    )


def solution(mesh):
    placed = (
        P(("dp", "tp"), None, None),
        P(("dp", "tp"), None, None),
        P(("dp", "tp"), None),
        P(("dp", "tp")),
        P(("dp", "tp")),
        P("dp", "tp", None),
        P(),
        P(),
    )
    return jax.shard_map(
        on_device,
        mesh=mesh,
        in_specs=placed,
        out_specs=P(("dp", "tp"), None, None),
        check_vma=False,
    )
```
